32 devices in a mesh: dp: 8 (over z, y), mp: 4 (over x, core).
Axes of the slice: x: 2, y: 2, z: 4, core: 2. Of those that a mesh axis runs over, the one named last changes fastest.
Arguments:
- table: float32 [65536, 512], P('dp', 'mp'), may hold values from -6 to 6
- first_moment: float32 [65536, 512], P('dp', 'mp'), may hold values from -1.8 to 1.8
- second_moment: float32 [65536, 512], P('dp', 'mp'), may hold values from 0.01 to 1
- grads: bfloat16 [16384, 512], P('dp', 'mp'), may hold values from -108 to 108
- ids: int32 [16384], P('dp'), may hold values from 0 to 65535, as said below
Outputs:
- new_table: float32 [65536, 512], P('dp', 'mp')
- new_first: float32 [65536, 512], P('dp', 'mp')
- new_second: float32 [65536, 512], P('dp', 'mp')
The draws below stay inside these ranges and needn't reach their ends.
Inputs may be any that keep to these rules, and one draw needn't show every extreme that they name: `ids`: the positions of one device name at most 1024 positions' worth of rows of any one owner (rows k * 8192 to (k + 1) * 8192 - 1) and at most 256 distinct rows of one owner; in every draw one owner reaches both bounds on every device.
All inputs are finite; a program needn't handle non-finite values.
Results may differ from the reference program's by a relative error of at most 0.0003.
Values may be sent and summed in bfloat16 or wider, within the bound.
No kernel may reach another device: no remote copies, remote signals or barrier semaphores. Data moves between devices by JAX's collectives and lax.ppermute only.
A program may use at most 64 MiB of HBM per device.

```python
import math
import jax
import jax.numpy as jnp

D = 512
ROWS_DEV = 8192
TOK_DEV = 2048
TOKENS = 16384
ROWS = 65536
N_DP = 8


def draw_grads(key, part):
    keys = jax.random.split(jax.random.fold_in(key, 11), 3)
    place = jnp.arange(TOKENS, dtype=jnp.float32)
    rising = 1.0 + 2.0 * place / (TOKENS - 1)
    noise = jnp.clip(jax.random.normal(keys[0], (TOKENS, D), jnp.float32), -4.0, 4.0)
    row_scale = jnp.exp(jax.random.uniform(keys[1], (TOKENS,), jnp.float32, math.log(0.3), math.log(3.0)))
    col_scale = jnp.exp(jax.random.uniform(keys[2], (D,), jnp.float32, math.log(0.3), math.log(3.0)))
    values = noise * (row_scale * rising)[:, None] * col_scale[None, :]
    return values.astype(jnp.bfloat16)


def draw_ids(key, part):
    keys = jax.random.split(jax.random.fold_in(key, 23), 7)
    room = TOK_DEV // N_DP
    most = 4 * room
    spread = ROWS_DEV // room
    owners = jnp.arange(N_DP, dtype=jnp.int32)
    hottest = jax.random.randint(keys[0], (), 0, N_DP, dtype=jnp.int32)
    jitter = jax.random.randint(keys[1], (N_DP, N_DP), 2, 4, dtype=jnp.int32)
    weight = (N_DP - 1 + 2 * owners)[None, :] * jitter
    is_hot = owners[None, :] == hottest
    weight = jnp.where(is_hot, 0, weight)
    spare = TOK_DEV - most
    counts = spare * weight // jnp.sum(weight, axis=1, keepdims=True)
    leftover = spare - jnp.sum(counts, axis=1, keepdims=True)
    ranking = jax.vmap(lambda k: jax.random.permutation(k, N_DP))(jax.random.split(keys[2], N_DP)).astype(jnp.int32)
    hot_rank = jnp.sum(jnp.where(is_hot, ranking, 0), axis=1, keepdims=True)
    adjusted = ranking - (ranking > hot_rank).astype(jnp.int32)
    extra = jnp.logical_and(jnp.logical_not(is_hot), adjusted < leftover)
    counts = counts + extra.astype(jnp.int32)
    counts = jnp.where(is_hot, most, counts)
    ends = jnp.cumsum(counts, axis=1)
    starts = ends - counts
    place = jnp.arange(TOK_DEV, dtype=jnp.int32)
    owner_of = jnp.sum((place[None, :, None] >= ends[:, None, :]).astype(jnp.int32), axis=2)
    within = place[None, :] - jnp.take_along_axis(starts, owner_of, axis=1)
    own_count = jnp.take_along_axis(counts, owner_of, axis=1)
    reach = jnp.maximum(jnp.minimum(room, (3 * own_count + 3) // 4), 1)
    guess = jax.random.randint(keys[3], (N_DP, TOK_DEV), 0, reach, dtype=jnp.int32)
    slot = jnp.where(within < reach, within, guess)
    shuffle = jax.vmap(lambda k: jax.random.permutation(k, room))(jax.random.split(keys[4], N_DP * N_DP)).astype(jnp.int32).reshape(N_DP, N_DP, room)
    offset = jax.random.randint(keys[5], (N_DP, N_DP, room), 0, spread, dtype=jnp.int32)
    device = jnp.arange(N_DP, dtype=jnp.int32)[:, None]
    local_row = shuffle[device, owner_of, slot] * spread + offset[device, owner_of, slot]
    rows = owner_of * ROWS_DEV + local_row
    mixing = jax.vmap(lambda k: jax.random.permutation(k, TOK_DEV))(jax.random.split(keys[6], N_DP)).astype(jnp.int32)
    rows = jnp.take_along_axis(rows, mixing, axis=1)
    return rows.reshape(TOKENS).astype(jnp.int32)


def block_scale(key, shape, cuts, least, largest):
    gain, own = 1.0, jax.random.fold_in(key, 6)
    for dim, shards_of in cuts:
        draws = jnp.exp(jax.random.uniform(jax.random.fold_in(own, dim), (shards_of,), jnp.float32, least / len(cuts), largest / len(cuts)))
        gain = gain * jnp.repeat(draws, shape[dim] // shards_of).reshape([-1 if axis == dim else 1 for axis in range(len(shape))])
    return gain


def bell_draw(stream_key, extent, scale, most, cuts=(), kind=jnp.bfloat16):
    entries = jax.random.normal(stream_key, extent, jnp.float32) * scale
    if len(cuts) > 0:
        entries = block_scale(stream_key, extent, cuts, -0.22, 0.18) * entries
    return jnp.clip(entries, min=-most, max=most).astype(kind)


def setup_inputs(seed: int = 0) -> dict:
    key_list = jax.random.split(jax.random.key(seed), 6)
    table = bell_draw(key_list[0], (ROWS, D), 1.0, 6.0, ((0, 8), (1, 4)), jnp.float32)
    first_moment = bell_draw(key_list[1], (ROWS, D), 0.3, 1.8, ((0, 8), (1, 4)), jnp.float32)
    second_moment = jnp.clip(jnp.exp(math.log(1.0) - 4.6051702 * jax.random.uniform(key_list[2], (ROWS, D), jnp.float32) ** block_scale(key_list[2], (ROWS, D), ((0, 8), (1, 4)), -0.2, 0.2)), 0.01, 1.0)
    grads = draw_grads(jax.random.fold_in(key_list[5], 71), 0)
    ids = draw_ids(jax.random.fold_in(key_list[5], 71), 0)
    return {"table": table, "first_moment": first_moment, "second_moment": second_moment, "grads": grads, "ids": ids}


first_fix = 0.9999734386
second_fix = 0.0952078529

def reference(table, first_moment, second_moment, grads, ids):
    grad_rows = jax.ops.segment_sum(grads.astype(jnp.float32), ids, num_segments=ROWS)
    total = jnp.sum(grad_rows * grad_rows)
    limit = jnp.sqrt(jnp.float32(TOKENS * D))
    scale = limit / jnp.maximum(jnp.sqrt(total), limit)
    clipped = scale * grad_rows
    new_first = 0.9 * first_moment + 0.1 * clipped
    new_second = 0.999 * second_moment + 0.001 * clipped * clipped
    first_hat = new_first / first_fix
    second_hat = new_second / second_fix
    new_table = table - 0.01 * (first_hat / (jnp.sqrt(second_hat) + 1e-08) + 0.1 * table)
    return (new_table, new_first, new_second)
```

```python
import functools
import math

import jax
import jax.numpy as jnp
from jax import lax
from jax.experimental import pallas as pl
from jax.experimental.pallas import tpu as pltpu
from jax.sharding import PartitionSpec as P

beta_first = 0.9
beta_second = 0.999
learn_rate = 0.01
decay_rate = 0.1
adam_eps = 1e-08
first_fix = 0.9999734386
second_fix = 0.0952078529

LANES = 128
META = 16
TOP = 32767.0
MIB = 2**20


def strip_rows(room):
    return -(-room // LANES)


def pack_kernel(peers, rows_dev, room, ids_ref, grads_ref, out_ref):
    tok = ids_ref.shape[1]
    per_owner = rows_dev // LANES
    buckets = peers * per_owner
    ids = ids_ref[...]
    high = ids // LANES
    low = ids - high * LANES
    f32, bf16 = jnp.float32, jnp.bfloat16

    def one_hot(keys, count):
        place = lax.broadcasted_iota(jnp.int32, (count, tok), 0)
        return jnp.where(place == keys, 1.0, 0.0).astype(bf16)

    high_hot = one_hot(high, buckets)
    low_hot = one_hot(low, LANES)
    counts = lax.dot_general(high_hot, low_hot, (((1,), (1,)), ((), ())), preferred_element_type=f32)
    present = jnp.where(counts > 0.0, 1.0, 0.0).astype(bf16)
    from_lane = lax.broadcasted_iota(jnp.int32, (LANES, LANES), 0)
    to_lane = lax.broadcasted_iota(jnp.int32, (LANES, LANES), 1)
    before = jnp.where(from_lane < to_lane, 1.0, 0.0).astype(bf16)
    within = jnp.dot(present, before, preferred_element_type=f32)
    totals = jnp.dot(present, jnp.ones((LANES, LANES), bf16), preferred_element_type=f32).astype(bf16)
    span = lax.broadcasted_iota(jnp.int32, (per_owner, per_owner), 0)
    other = lax.broadcasted_iota(jnp.int32, (per_owner, per_owner), 1)
    earlier = jnp.where(other < span, 1.0, 0.0).astype(bf16)
    offsets = [
        jnp.dot(earlier, totals[o * per_owner : (o + 1) * per_owner], preferred_element_type=f32)
        for o in range(peers)
    ]
    ranks = within + jnp.concatenate(offsets, axis=0)
    by_low = jnp.dot(ranks.T.astype(bf16), high_hot, preferred_element_type=f32)
    rank = jnp.sum(by_low * low_hot.astype(f32), axis=0, keepdims=True)
    rank = rank.astype(jnp.int32)

    sub = lax.broadcasted_iota(jnp.int32, (8, tok), 0)
    local_high = lax.rem(high, per_owner)
    digits = jnp.where(sub == 0, local_high, jnp.where(sub == 1, low, jnp.where(sub == 2, 1, 0)))
    digits = digits.astype(f32)
    aux = []
    for c in range(tok // LANES):
        tile = digits[:, c * LANES : (c + 1) * LANES]
        tile = jnp.concatenate([tile, jnp.zeros((LANES - 8, LANES), f32)], axis=0)
        aux.append(tile.T)
    wide = jnp.concatenate([grads_ref[...], jnp.concatenate(aux, axis=0).astype(bf16)], axis=1)

    lane = lax.broadcasted_iota(jnp.int32, (room, LANES), 1)
    meta = jnp.zeros((room, LANES), f32)
    for o in range(peers):
        inside = jnp.logical_and(ids >= o * rows_dev, ids < (o + 1) * rows_dev)
        match = one_hot(jnp.where(inside, rank, -1), room)
        summed = jnp.dot(match, wide, preferred_element_type=f32)
        sums = summed[:, :LANES]
        number = summed[:, LANES + 2 : LANES + 3]
        digit_high = summed[:, LANES : LANES + 1]
        digit_low = summed[:, LANES + 1 : LANES + 2]
        mark = jnp.where(
            number > 0.0,
            jnp.floor((digit_high * LANES + digit_low) / jnp.maximum(number, 1.0) + 0.5),
            float(rows_dev),
        )
        largest = jnp.max(jnp.abs(sums), axis=1, keepdims=True)
        power = jnp.ceil(jnp.log2(jnp.maximum(largest, 1e-30) * (1.0 / TOP)))
        code = jnp.clip(jnp.round(sums * jnp.exp2(-power)), -TOP, TOP)
        out_ref[o, :room, :] = code.astype(jnp.int32).astype(jnp.int16)
        meta = jnp.where(lane == 2 * o, mark, jnp.where(lane == 2 * o + 1, power, meta))
    strips = strip_rows(room)
    flat = meta.T.astype(jnp.int32)
    for o in range(peers):
        rows = []
        for k in range(2):
            for c in range(strips):
                piece = flat[2 * o + k : 2 * o + k + 1, c * LANES : min((c + 1) * LANES, room)]
                if piece.shape[1] < LANES:
                    piece = jnp.concatenate([piece, jnp.zeros((1, LANES - piece.shape[1]), jnp.int32)], axis=1)
                rows.append(piece)
        rows.append(jnp.zeros((META - len(rows), LANES), jnp.int32))
        out_ref[o, room:, :] = jnp.concatenate(rows, axis=0).astype(jnp.int16)


def add_kernel(peers, rows_dev, room, got_ref, acc_ref, part_ref, marks, values, slots, sem):
    strips = strip_rows(room)
    f32 = jnp.float32
    mark_rows, power_rows = [], []
    for s in range(peers):
        meta = got_ref[s, room:, :].astype(jnp.int32)
        mark_rows.append(meta[0:strips])
        power_rows.append(meta[strips : 2 * strips])
    marks[...] = jnp.concatenate(mark_rows, axis=0)
    copy = pltpu.make_async_copy(marks, slots, sem)
    copy.start()
    acc_ref[...] = jnp.zeros_like(acc_ref)
    powers = jnp.concatenate(power_rows, axis=0).astype(f32)
    count = powers.shape[0]
    padded = -(-count // LANES) * LANES
    if padded > count:
        powers = jnp.concatenate([powers, jnp.zeros((padded - count, LANES), f32)], axis=0)
    scales = jnp.exp2(powers).T
    for s in range(peers):
        for c in range(strips):
            high = min(LANES, room - c * LANES)
            code = got_ref[s, c * LANES : c * LANES + high, :].astype(jnp.int32).astype(f32)
            column = s * strips + c
            values[s * room + c * LANES : s * room + c * LANES + high, :] = code * scales[:high, column : column + 1]
    copy.wait()
    batch = 16
    per_strip = min(room, LANES) // batch

    def step(i, carry):
        strip = i // per_strip
        first = (i - strip * per_strip) * batch
        spots = [slots[strip, first + k] for k in range(batch)]
        base = pl.multiple_of(i * batch, batch)
        adds = [acc_ref[pl.ds(spots[k], 1), :] + values[pl.ds(base + k, 1), :] for k in range(batch)]
        for k in range(batch):
            acc_ref[pl.ds(spots[k], 1), :] = adds[k]
        return carry

    lax.fori_loop(0, peers * room // batch, step, 0)

    def square(i, total):
        block = acc_ref[pl.ds(pl.multiple_of(i * LANES, LANES), LANES), :]
        return total + jnp.sum((block * block).reshape(LANES // 8, 8, LANES), axis=0)

    total = lax.fori_loop(0, rows_dev // LANES, square, jnp.zeros((8, LANES), f32))
    total = jnp.sum(total, axis=0, keepdims=True)
    total = jnp.sum(total, axis=1, keepdims=True)
    part_ref[...] = jnp.broadcast_to(total[None], part_ref.shape)


def update_kernel(limit, parts_ref, grad_ref, table_ref, first_ref, second_ref, table_out, first_out, second_out, scale_ref):
    @pl.when(pl.program_id(0) == 0)
    def _():
        total = jnp.sum(parts_ref[...], axis=0)
        scale_ref[...] = limit / jnp.maximum(jnp.sqrt(total), limit)

    clipped = scale_ref[...] * grad_ref[...]
    new_first = beta_first * first_ref[...] + (1.0 - beta_first) * clipped
    new_second = beta_second * second_ref[...] + (1.0 - beta_second) * clipped * clipped
    first_hat = new_first / first_fix
    second_hat = new_second / second_fix
    table = table_ref[...]
    table_out[...] = table - learn_rate * (first_hat / (jnp.sqrt(second_hat) + adam_eps) + decay_rate * table)
    first_out[...] = new_first
    second_out[...] = new_second


def body(table, first_moment, second_moment, grads, ids):
    peers = lax.axis_size("dp")
    everyone = peers * lax.axis_size("mp")
    rows_dev, width = table.shape
    tok_dev = grads.shape[0]
    room = tok_dev // peers
    f32 = jnp.float32
    whole = pl.BlockSpec(memory_space=pltpu.VMEM)
    packed = pl.pallas_call(
        functools.partial(pack_kernel, peers, rows_dev, room),
        out_shape=jax.ShapeDtypeStruct((peers, room + META, width), jnp.int16),
        in_specs=[whole, whole],
        out_specs=whole,
        compiler_params=pltpu.CompilerParams(vmem_limit_bytes=40 * MIB),
        name="pack_rows",
    )(ids.reshape(1, tok_dev), grads)
    got = lax.all_to_all(packed, "dp", split_axis=0, concat_axis=0, tiled=True)
    strips = strip_rows(room)
    grad_rows, part = pl.pallas_call(
        functools.partial(add_kernel, peers, rows_dev, room),
        out_shape=(
            jax.ShapeDtypeStruct((rows_dev + 8, width), f32),
            jax.ShapeDtypeStruct((everyone, 1, width), f32),
        ),
        in_specs=[whole],
        out_specs=(whole, whole),
        scratch_shapes=[
            pltpu.VMEM((peers * strips, LANES), jnp.int32),
            pltpu.VMEM((peers * room, width), f32),
            pltpu.SMEM((peers * strips, LANES), jnp.int32),
            pltpu.SemaphoreType.DMA,
        ],
        compiler_params=pltpu.CompilerParams(vmem_limit_bytes=32 * MIB),
        name="add_rows",
    )(got)
    parts = lax.all_to_all(part, ("dp", "mp"), split_axis=0, concat_axis=0, tiled=True)
    limit = math.sqrt(tok_dev * everyone * width)
    step = 1024
    block = pl.BlockSpec((step, width), lambda i: (i, 0))
    return pl.pallas_call(
        functools.partial(update_kernel, limit),
        out_shape=tuple(jax.ShapeDtypeStruct((rows_dev, width), f32) for _ in range(3)),
        grid=(rows_dev // step,),
        in_specs=[pl.BlockSpec((everyone, 1, width), lambda i: (0, 0, 0)), block, block, block, block],
        out_specs=(block, block, block),
        scratch_shapes=[pltpu.VMEM((1, width), f32)],
        compiler_params=pltpu.CompilerParams(vmem_limit_bytes=24 * MIB),
        name="update_rows",
    )(parts, grad_rows, table, first_moment, second_moment)


def solution(mesh):
    in_specs = (P("dp", "mp"), P("dp", "mp"), P("dp", "mp"), P("dp", "mp"), P("dp"))
    out_specs = (P("dp", "mp"), P("dp", "mp"), P("dp", "mp"))
    return jax.shard_map(body, mesh=mesh, in_specs=in_specs, out_specs=out_specs, check_vma=False)
```

```python
import functools
import math

import jax
import jax.numpy as jnp
from jax import lax
from jax.experimental import pallas as pl
from jax.experimental.pallas import tpu as pltpu
from jax.sharding import PartitionSpec as P

beta_first = 0.9
beta_second = 0.999
learn_rate = 0.01
decay_rate = 0.1
adam_eps = 1e-08
first_fix = 0.9999734386
second_fix = 0.0952078529

LANES = 128
META = 16
TOP = 32767.0
MIB = 2**20


def strip_rows(room):
    return -(-room // LANES)


def partner(me, hop, peers):
    return me ^ hop if peers & (peers - 1) == 0 else lax.rem(me + hop, peers)


def pack_kernel(peers, rows_dev, room, ids_hbm, grads_hbm, table_hbm, first_hbm, second_hbm, *refs):
    outs, refs = refs[:peers], refs[peers:]
    table_ref, first_ref, second_ref, ids_ref, grads_ref, sems = refs
    pairs = (
        (ids_hbm, ids_ref),
        (grads_hbm, grads_ref),
        (table_hbm, table_ref),
        (first_hbm, first_ref),
        (second_hbm, second_ref),
    )
    copies = [pltpu.make_async_copy(a, b, sems.at[n]) for n, (a, b) in enumerate(pairs)]
    for copy in copies:
        copy.start()
    me = lax.axis_index("dp")
    copies[0].wait()
    tok = ids_ref.shape[1]
    per_owner = rows_dev // LANES
    buckets = peers * per_owner
    ids = ids_ref[...]
    high = ids // LANES
    low = ids - high * LANES
    f32, bf16 = jnp.float32, jnp.bfloat16

    def one_hot(keys, count):
        place = lax.broadcasted_iota(jnp.int32, (count, tok), 0)
        return jnp.where(place == keys, 1.0, 0.0).astype(bf16)

    high_hot = one_hot(high, buckets)
    low_hot = one_hot(low, LANES)
    counts = lax.dot_general(high_hot, low_hot, (((1,), (1,)), ((), ())), preferred_element_type=f32)
    present = jnp.where(counts > 0.0, 1.0, 0.0).astype(bf16)
    from_lane = lax.broadcasted_iota(jnp.int32, (LANES, LANES), 0)
    to_lane = lax.broadcasted_iota(jnp.int32, (LANES, LANES), 1)
    before = jnp.where(from_lane < to_lane, 1.0, 0.0).astype(bf16)
    within = jnp.dot(present, before, preferred_element_type=f32)
    totals = jnp.dot(present, jnp.ones((LANES, LANES), bf16), preferred_element_type=f32).astype(bf16)
    span = lax.broadcasted_iota(jnp.int32, (per_owner, per_owner), 0)
    other = lax.broadcasted_iota(jnp.int32, (per_owner, per_owner), 1)
    earlier = jnp.where(other < span, 1.0, 0.0).astype(bf16)
    offsets = [
        jnp.dot(earlier, totals[o * per_owner : (o + 1) * per_owner], preferred_element_type=f32)
        for o in range(peers)
    ]
    ranks = within + jnp.concatenate(offsets, axis=0)
    by_low = jnp.dot(ranks.T.astype(bf16), high_hot, preferred_element_type=f32)
    rank = jnp.sum(by_low * low_hot.astype(f32), axis=0, keepdims=True)
    rank = rank.astype(jnp.int32)

    sub = lax.broadcasted_iota(jnp.int32, (8, tok), 0)
    local_high = lax.rem(high, per_owner)
    digits = jnp.where(sub == 0, local_high, jnp.where(sub == 1, low, jnp.where(sub == 2, 1, 0)))
    digits = digits.astype(f32)
    aux = []
    for c in range(tok // LANES):
        tile = digits[:, c * LANES : (c + 1) * LANES]
        tile = jnp.concatenate([tile, jnp.zeros((LANES - 8, LANES), f32)], axis=0)
        aux.append(tile.T)
    copies[1].wait()
    wide = jnp.concatenate([grads_ref[...], jnp.concatenate(aux, axis=0).astype(bf16)], axis=1)

    lane = lax.broadcasted_iota(jnp.int32, (room, LANES), 1)
    meta = jnp.zeros((room, LANES), f32)
    for o in range(peers):
        low_id = partner(me, o, peers) * rows_dev
        inside = jnp.logical_and(ids >= low_id, ids < low_id + rows_dev)
        match = one_hot(jnp.where(inside, rank, -1), room)
        summed = jnp.dot(match, wide, preferred_element_type=f32)
        sums = summed[:, :LANES]
        number = summed[:, LANES + 2 : LANES + 3]
        digit_high = summed[:, LANES : LANES + 1]
        digit_low = summed[:, LANES + 1 : LANES + 2]
        mark = jnp.where(
            number > 0.0,
            jnp.floor((digit_high * LANES + digit_low) / jnp.maximum(number, 1.0) + 0.5),
            float(rows_dev),
        )
        largest = jnp.max(jnp.abs(sums), axis=1, keepdims=True)
        power = jnp.ceil(jnp.log2(jnp.maximum(largest, 1e-30) * (1.0 / TOP)))
        code = jnp.clip(jnp.round(sums * jnp.exp2(-power)), -TOP, TOP)
        outs[o][:room, :] = code.astype(jnp.int32).astype(jnp.int16)
        meta = jnp.where(lane == 2 * o, mark, jnp.where(lane == 2 * o + 1, power, meta))
    strips = strip_rows(room)
    flat = meta.T.astype(jnp.int32)
    for o in range(peers):
        rows = []
        for k in range(2):
            for c in range(strips):
                piece = flat[2 * o + k : 2 * o + k + 1, c * LANES : min((c + 1) * LANES, room)]
                if piece.shape[1] < LANES:
                    piece = jnp.concatenate([piece, jnp.zeros((1, LANES - piece.shape[1]), jnp.int32)], axis=1)
                rows.append(piece)
        rows.append(jnp.zeros((META - len(rows), LANES), jnp.int32))
        outs[o][room:, :] = jnp.concatenate(rows, axis=0).astype(jnp.int16)
    for copy in copies[2:]:
        copy.wait()


def join_kernel(peers, room, *refs):
    got, refs = refs[:peers], refs[peers:]
    grad_ref, part_ref, wide, sums_buf, marks_buf, slots, sem = refs
    strips = strip_rows(room)
    f32, bf16 = jnp.float32, jnp.bfloat16
    lines = peers * strips
    strip = min(room, LANES)
    mark_rows, power_rows = [], []
    for s in range(peers):
        meta = got[s][room:, :].astype(jnp.int32)
        mark_rows.append(meta[0:strips])
        power_rows.append(meta[strips : 2 * strips])
    marks = jnp.concatenate(mark_rows, axis=0)
    marks_buf[...] = marks
    copy = pltpu.make_async_copy(marks_buf, slots, sem)
    copy.start()
    grad_ref[...] = jnp.zeros_like(grad_ref)
    fill = jnp.zeros((LANES - 2 * lines, LANES), jnp.int32)
    both = jnp.concatenate([marks] + power_rows + [fill], axis=0).astype(f32)
    columns = both.T
    mark_columns = columns.astype(jnp.int32)
    scale_columns = jnp.exp2(columns)
    mark_line = jnp.concatenate([marks[k : k + 1, :strip] for k in range(lines)], axis=1)
    power_line = jnp.concatenate([both[lines + k : lines + k + 1, :strip] for k in range(lines)], axis=1)
    scale_line = jnp.exp2(power_line)
    for s in range(peers):
        code = got[s][:room, :].astype(jnp.int32)
        upper = (code + 128) >> 8
        lower = code - upper * 256
        halves = jnp.concatenate([upper.astype(f32), lower.astype(f32)], axis=1)
        wide[s * room : (s + 1) * room, :] = halves.astype(bf16)
    total = jnp.zeros((8, LANES), f32)
    per_block = max(1, min(256, peers * room) // strip)
    for first in range(0, lines, per_block):
        block = range(first, min(first + per_block, lines))
        same = [jnp.where(mark_columns[:strip, k : k + 1] == mark_line, scale_line, 0.0).astype(bf16) for k in block]
        sums = jnp.dot(jnp.concatenate(same, axis=0), wide[...], preferred_element_type=f32)
        sums = sums[:, :LANES] * 256.0 + sums[:, LANES:]
        sums_buf[first * strip : first * strip + len(block) * strip, :] = sums
        for n, k in enumerate(block):
            own = wide[k * strip : (k + 1) * strip, :].astype(f32)
            own = (own[:, :LANES] * 256.0 + own[:, LANES:]) * scale_columns[:strip, lines + k : lines + k + 1]
            product = own * sums[n * strip : (n + 1) * strip]
            total = total + jnp.sum(product.reshape(strip // 8, 8, LANES), axis=0)
        if first == 0:
            copy.wait()
        for k in block:
            for r in range(strip):
                grad_ref[pl.ds(slots[k, r], 1), :] = sums_buf[k * strip + r : k * strip + r + 1, :]
    total = jnp.sum(total, axis=0, keepdims=True)
    total = jnp.sum(total, axis=1, keepdims=True)
    part_ref[...] = jnp.broadcast_to(total[None], part_ref.shape)


def update_kernel(limit, step, parts_ref, grad_ref, table_ref, first_ref, second_ref, table_out, first_out, second_out,
                  table_buf, first_buf, second_buf, sems):
    total = jnp.sum(parts_ref[...], axis=0)
    scale = limit / jnp.maximum(jnp.sqrt(total), limit)
    rows = table_ref.shape[0]
    copies = []
    for n in range(rows // step):
        part = pl.ds(n * step, step)
        clipped = scale * grad_ref[part, :]
        new_first = beta_first * first_ref[part, :] + (1.0 - beta_first) * clipped
        first_buf[part, :] = new_first
        new_second = beta_second * second_ref[part, :] + (1.0 - beta_second) * clipped * clipped
        second_buf[part, :] = new_second
        change = (new_first * (learn_rate / first_fix)) / (jnp.sqrt(new_second * (1.0 / second_fix)) + adam_eps)
        table_buf[part, :] = table_ref[part, :] * (1.0 - learn_rate * decay_rate) - change
        for k, (a, b) in enumerate(((first_buf, first_out), (second_buf, second_out), (table_buf, table_out))):
            copy = pltpu.make_async_copy(a.at[part], b.at[part], sems.at[k, n])
            copy.start()
            copies.append(copy)
    for copy in copies:
        copy.wait()


def body(table, first_moment, second_moment, grads, ids):
    peers = lax.axis_size("dp")
    everyone = peers * lax.axis_size("mp")
    rows_dev, width = table.shape
    tok_dev = grads.shape[0]
    room = tok_dev // peers
    strips = strip_rows(room)
    f32 = jnp.float32
    shape = jax.ShapeDtypeStruct
    vmem = pl.BlockSpec(memory_space=pltpu.VMEM)
    hbm = pl.BlockSpec(memory_space=pltpu.HBM)
    in_hbm = lambda x: pltpu.with_memory_space_constraint(x, pltpu.HBM)
    in_vmem = lambda x: pltpu.with_memory_space_constraint(x, pltpu.VMEM)
    kept = pltpu.VMEM((rows_dev, width), f32)
    dense = shape((rows_dev, width), f32)
    *packed, table_kept, first_kept, second_kept = pl.pallas_call(
        functools.partial(pack_kernel, peers, rows_dev, room),
        out_shape=(shape((room + META, width), jnp.int16),) * peers + (kept,) * 3,
        in_specs=[hbm] * 5,
        out_specs=(vmem,) * (peers + 3),
        scratch_shapes=[
            pltpu.VMEM((1, tok_dev), jnp.int32),
            pltpu.VMEM((tok_dev, width), jnp.bfloat16),
            pltpu.SemaphoreType.DMA((5,)),
        ],
        compiler_params=pltpu.CompilerParams(vmem_limit_bytes=24 * MIB),
        name="pack_rows",
    )(*[in_hbm(x) for x in (ids.reshape(1, tok_dev), grads, table, first_moment, second_moment)])
    got = [packed[0]] + [None] * (peers - 1)
    for hop in range(peers - 1, 0, -1):
        pairs = [(i, int(partner(i, hop, peers)) if peers & (peers - 1) == 0 else (i + hop) % peers) for i in range(peers)]
        got[hop] = lax.ppermute(packed[hop], "dp", pairs)
    grad_rows, part = pl.pallas_call(
        functools.partial(join_kernel, peers, room),
        out_shape=(pltpu.VMEM((rows_dev + 8, width), f32), shape((everyone, 1, width), f32)),
        in_specs=[vmem] * peers,
        out_specs=(vmem,) * 2,
        scratch_shapes=[
            pltpu.VMEM((peers * room, 2 * width), jnp.bfloat16),
            pltpu.VMEM((peers * room, width), f32),
            pltpu.VMEM((peers * strips, LANES), jnp.int32),
            pltpu.SMEM((peers * strips, LANES), jnp.int32),
            pltpu.SemaphoreType.DMA,
        ],
        compiler_params=pltpu.CompilerParams(vmem_limit_bytes=16 * MIB),
        name="join_rows",
    )(got[0], *got[:0:-1])
    parts = lax.all_to_all(part, ("dp", "mp"), split_axis=0, concat_axis=0, tiled=True)
    limit = math.sqrt(tok_dev * everyone * width)
    step = math.gcd(1024, rows_dev)
    return pl.pallas_call(
        functools.partial(update_kernel, limit, step),
        out_shape=(dense,) * 3,
        in_specs=[vmem] * 5,
        out_specs=(hbm,) * 3,
        scratch_shapes=[pltpu.VMEM((rows_dev, width), f32)] * 3 + [pltpu.SemaphoreType.DMA((3, rows_dev // step))],
        compiler_params=pltpu.CompilerParams(vmem_limit_bytes=20 * MIB),
        name="update_rows",
    )(parts, *[in_vmem(x) for x in (grad_rows, table_kept, first_kept, second_kept)])


def solution(mesh):
    in_specs = (P("dp", "mp"), P("dp", "mp"), P("dp", "mp"), P("dp", "mp"), P("dp"))
    out_specs = (P("dp", "mp"), P("dp", "mp"), P("dp", "mp"))
    return jax.shard_map(body, mesh=mesh, in_specs=in_specs, out_specs=out_specs, check_vma=False)
```

```python
import functools
import math

import jax
import jax.numpy as jnp
from jax import lax
from jax.experimental import pallas as pl
from jax.experimental.pallas import tpu as pltpu
from jax.sharding import PartitionSpec as P

beta_first = 0.9
beta_second = 0.999
learn_rate = 0.01
decay_rate = 0.1
adam_eps = 1e-08
first_fix = 0.9999734386
second_fix = 0.0952078529

LANES = 128
META = 16
TOP = 32767.0
MIB = 2**20


def strip_rows(room):
    return -(-room // LANES)


def relative(me, owner, peers):
    return owner ^ me if peers & (peers - 1) == 0 else lax.rem(owner - me + peers, peers)


def hop_pairs(hop, peers):
    return [(i, i ^ hop if peers & (peers - 1) == 0 else (i + hop) % peers) for i in range(peers)]


def one_hot(keys, count):
    place = lax.broadcasted_iota(jnp.int32, (count, keys.shape[1]), 0)
    return jnp.where(place == keys, 1.0, 0.0).astype(jnp.bfloat16)


def slot_ranks(rel, group, rows_dev):
    f32, bf16 = jnp.float32, jnp.bfloat16
    per_owner = rows_dev // LANES
    high = rel >> 7
    low = rel & (LANES - 1)
    high_hot = one_hot(high, group * per_owner)
    low_hot = one_hot(low, LANES)
    counts = lax.dot_general(high_hot, low_hot, (((1,), (1,)), ((), ())), preferred_element_type=f32)
    present = jnp.where(counts > 0.0, 1.0, 0.0).astype(bf16)
    from_lane = lax.broadcasted_iota(jnp.int32, (LANES, LANES), 0)
    to_lane = lax.broadcasted_iota(jnp.int32, (LANES, LANES), 1)
    before = jnp.where(from_lane < to_lane, 1.0, 0.0).astype(bf16)
    within = jnp.dot(present, before, preferred_element_type=f32)
    totals = jnp.dot(present, jnp.ones((LANES, LANES), bf16), preferred_element_type=f32).astype(bf16)
    span = lax.broadcasted_iota(jnp.int32, (per_owner, per_owner), 0)
    other = lax.broadcasted_iota(jnp.int32, (per_owner, per_owner), 1)
    earlier = jnp.where(other < span, 1.0, 0.0).astype(bf16)
    offsets = [
        jnp.dot(earlier, totals[o * per_owner : (o + 1) * per_owner], preferred_element_type=f32)
        for o in range(group)
    ]
    ranks = within + jnp.concatenate(offsets, axis=0)
    by_low = jnp.dot(ranks.T.astype(bf16), high_hot, preferred_element_type=f32)
    return jnp.sum(by_low * low_hot.astype(f32), axis=0, keepdims=True).astype(jnp.int32)


def pack_group(rel, rank, wide, first, outs, rows_dev, room):
    f32 = jnp.float32
    group = len(outs)
    strips = strip_rows(room)
    lane = lax.broadcasted_iota(jnp.int32, (room, LANES), 1)
    meta = jnp.zeros((room, LANES), f32)
    for o in range(group):
        inside = jnp.logical_and(rel >= (first + o) * rows_dev, rel < (first + o + 1) * rows_dev)
        match = one_hot(jnp.where(inside, rank, -1), room)
        summed = jnp.dot(match, wide, preferred_element_type=f32)
        sums = summed[:, :LANES]
        digit_high = summed[:, LANES : LANES + 1]
        digit_low = summed[:, LANES + 1 : LANES + 2]
        number = summed[:, LANES + 2 : LANES + 3]
        mark = jnp.where(
            number > 0.0,
            jnp.floor((digit_high * LANES + digit_low) / jnp.maximum(number, 1.0) + 0.5),
            float(rows_dev),
        )
        largest = jnp.max(jnp.abs(sums), axis=1, keepdims=True)
        power = jnp.ceil(jnp.log2(jnp.maximum(largest, 1e-30) * (1.0 / TOP)))
        code = jnp.clip(jnp.round(sums * jnp.exp2(-power)), -TOP, TOP)
        outs[o][:room, :] = code.astype(jnp.int32).astype(jnp.int16)
        meta = jnp.where(lane == 2 * o, mark, jnp.where(lane == 2 * o + 1, power, meta))
    flat = meta.T.astype(jnp.int32)
    for o in range(group):
        rows = []
        for k in range(2):
            for c in range(strips):
                piece = flat[2 * o + k : 2 * o + k + 1, c * LANES : min((c + 1) * LANES, room)]
                if piece.shape[1] < LANES:
                    piece = jnp.concatenate([piece, jnp.zeros((1, LANES - piece.shape[1]), jnp.int32)], axis=1)
                rows.append(piece)
        rows.append(jnp.zeros((META - len(rows), LANES), jnp.int32))
        outs[o][room:, :] = jnp.concatenate(rows, axis=0).astype(jnp.int16)


def low_part(ids, size):
    return ids & (size - 1) if size & (size - 1) == 0 else lax.rem(ids, size)


def relative_rows(ids, peers, rows_dev):
    me = lax.axis_index("dp")
    if rows_dev & (rows_dev - 1) == 0 and peers & (peers - 1) == 0:
        return ids ^ (me * rows_dev)
    owner = ids // rows_dev
    return relative(me, owner, peers) * rows_dev + (ids - owner * rows_dev)


def pack_far_kernel(peers, rows_dev, room, ids_hbm, grads_hbm, table_hbm, first_hbm, *refs):
    far = peers - peers // 2
    outs, refs = refs[:far], refs[far:]
    rel_ref, rank_ref, wide_ref, table_ref, first_ref, ids_ref, grads_ref, sems = refs
    pairs = ((ids_hbm, ids_ref), (grads_hbm, grads_ref), (table_hbm, table_ref), (first_hbm, first_ref))
    copies = [pltpu.make_async_copy(a, b, sems.at[n]) for n, (a, b) in enumerate(pairs)]
    for copy in copies:
        copy.start()
    copies[0].wait()
    rel = relative_rows(ids_ref[...], peers, rows_dev)
    tok = rel.shape[1]
    rank = slot_ranks(rel, peers, rows_dev)
    rel_ref[...] = rel
    rank_ref[...] = rank
    sub = lax.broadcasted_iota(jnp.int32, (8, tok), 0)
    high = low_part(rel, rows_dev) >> 7
    low = rel & (LANES - 1)
    digits = jnp.where(sub == 0, high, jnp.where(sub == 1, low, jnp.where(sub == 2, 1, 0))).astype(jnp.float32)
    aux = []
    for c in range(tok // LANES):
        tile = digits[:, c * LANES : (c + 1) * LANES]
        tile = jnp.concatenate([tile, jnp.zeros((LANES - 8, LANES), jnp.float32)], axis=0)
        aux.append(tile.T)
    copies[1].wait()
    wide = jnp.concatenate([grads_ref[...], jnp.concatenate(aux, axis=0).astype(jnp.bfloat16)], axis=1)
    wide_ref[...] = wide
    pack_group(rel, rank, wide, peers // 2, outs, rows_dev, room)
    for copy in copies[2:]:
        copy.wait()


def pack_near_kernel(peers, rows_dev, room, rel_ref, rank_ref, wide_ref, second_hbm, *refs):
    outs, (second_ref, sem) = refs[: peers // 2], refs[peers // 2 :]
    copy = pltpu.make_async_copy(second_hbm, second_ref, sem)
    copy.start()
    pack_group(rel_ref[...], rank_ref[...], wide_ref[...], 0, outs, rows_dev, room)
    copy.wait()


def open_blocks(got, room, marks_buf, slots, sem, wide):
    strips = strip_rows(room)
    f32, bf16 = jnp.float32, jnp.bfloat16
    lines = len(got) * strips
    strip = min(room, LANES)
    mark_rows, power_rows = [], []
    for ref in got:
        meta = ref[room:, :].astype(jnp.int32)
        mark_rows.append(meta[0:strips])
        power_rows.append(meta[strips : 2 * strips])
    marks = jnp.concatenate(mark_rows, axis=0)
    marks_buf[...] = marks
    copy = pltpu.make_async_copy(marks_buf, slots, sem)
    copy.start()
    fill = jnp.zeros((LANES - 2 * lines, LANES), jnp.int32)
    both = jnp.concatenate([marks] + power_rows + [fill], axis=0).astype(f32)
    columns = both.T
    mark_columns = columns.astype(jnp.int32)
    scale_columns = jnp.exp2(columns)
    mark_line = jnp.concatenate([marks[k : k + 1, :strip] for k in range(lines)], axis=1)
    power_line = jnp.concatenate([both[lines + k : lines + k + 1, :strip] for k in range(lines)], axis=1)
    scale_line = jnp.exp2(power_line)
    for s, ref in enumerate(got):
        code = ref[:room, :].astype(jnp.int32)
        upper = (code + 128) >> 8
        lower = code - upper * 256
        halves = jnp.concatenate([upper.astype(f32), lower.astype(f32)], axis=1)
        wide[s * room : (s + 1) * room, :] = halves.astype(bf16)
    return copy, lines, strip, mark_line, scale_line, mark_columns, scale_columns


def block_sums(block, strip, mark_line, scale_line, mark_columns, wide):
    same = [
        jnp.where(mark_columns[:strip, k : k + 1] == mark_line, scale_line, 0.0).astype(jnp.bfloat16) for k in block
    ]
    sums = jnp.dot(jnp.concatenate(same, axis=0), wide[...], preferred_element_type=jnp.float32)
    return sums[:, :LANES] * 256.0 + sums[:, LANES:]


def own_rows(k, strip, lines, scale_columns, wide):
    own = wide[k * strip : (k + 1) * strip, :].astype(jnp.float32)
    return (own[:, :LANES] * 256.0 + own[:, LANES:]) * scale_columns[:strip, lines + k : lines + k + 1]


def fold(product):
    return jnp.sum(product.reshape(product.shape[0] // 8, 8, LANES), axis=0)


def line_blocks(lines, strip):
    per_block = max(1, 256 // strip)
    return [range(k, min(k + per_block, lines)) for k in range(0, lines, per_block)]


def join_kernel(group, room, opens, ends, *refs):
    got, refs = refs[:group], refs[group:]
    if not opens:
        (_, sum_ref), refs = refs[:2], refs[2:]
    grad_ref, part_ref, wide, sums_buf, before_buf, marks_buf, slots, sem = refs
    if opens:
        grad_ref[...] = jnp.zeros_like(grad_ref)
    copy, lines, strip, mark_line, scale_line, mark_columns, scale_columns = open_blocks(
        got, room, marks_buf, slots, sem, wide
    )
    total = jnp.zeros((8, LANES), jnp.float32) if opens else sum_ref[...]
    if not opens:
        copy.wait()
        for k in range(lines):
            for r in range(strip):
                before_buf[k * strip + r : k * strip + r + 1, :] = grad_ref[pl.ds(slots[k, r], 1), :]
    for block in line_blocks(lines, strip):
        sums = block_sums(block, strip, mark_line, scale_line, mark_columns, wide)
        for n, k in enumerate(block):
            here = slice(k * strip, (k + 1) * strip)
            after = sums[n * strip : (n + 1) * strip]
            twice = after
            if not opens:
                before = before_buf[here, :]
                after = before + after
                twice = before + after
            sums_buf[here, :] = after
            total = total + fold(own_rows(k, strip, lines, scale_columns, wide) * twice)
        if opens and block[0] == 0:
            copy.wait()
        for k in block:
            for r in range(strip):
                grad_ref[pl.ds(slots[k, r], 1), :] = sums_buf[k * strip + r : k * strip + r + 1, :]
    if ends:
        total = jnp.sum(total, axis=0, keepdims=True)
        total = jnp.sum(total, axis=1, keepdims=True)
        part_ref[...] = jnp.broadcast_to(total[None], part_ref.shape)
    else:
        part_ref[...] = total


def update_kernel(limit, step, parts_ref, grad_ref, table_ref, first_ref, second_ref, table_out, first_out, second_out,
                  table_buf, first_buf, second_buf, sems):
    total = jnp.sum(parts_ref[...], axis=0)
    scale = limit / jnp.maximum(jnp.sqrt(total), limit)
    rows = table_ref.shape[0]
    copies = []
    for n in range(rows // step):
        part = pl.ds(n * step, step)
        clipped = scale * grad_ref[part, :]
        new_first = beta_first * first_ref[part, :] + (1.0 - beta_first) * clipped
        first_buf[part, :] = new_first
        new_second = beta_second * second_ref[part, :] + (1.0 - beta_second) * clipped * clipped
        second_buf[part, :] = new_second
        change = (new_first * (learn_rate / first_fix)) / (jnp.sqrt(new_second * (1.0 / second_fix)) + adam_eps)
        table_buf[part, :] = table_ref[part, :] * (1.0 - learn_rate * decay_rate) - change
        for k, (a, b) in enumerate(((first_buf, first_out), (second_buf, second_out), (table_buf, table_out))):
            copy = pltpu.make_async_copy(a.at[part], b.at[part], sems.at[k, n])
            copy.start()
            copies.append(copy)
    for copy in copies:
        copy.wait()


def body(table, first_moment, second_moment, grads, ids):
    peers = lax.axis_size("dp")
    everyone = peers * lax.axis_size("mp")
    rows_dev, width = table.shape
    tok_dev = grads.shape[0]
    room = tok_dev // peers
    strips = strip_rows(room)
    f32 = jnp.float32
    shape = jax.ShapeDtypeStruct
    vmem = pl.BlockSpec(memory_space=pltpu.VMEM)
    hbm = pl.BlockSpec(memory_space=pltpu.HBM)
    in_hbm = lambda x: pltpu.with_memory_space_constraint(x, pltpu.HBM)
    in_vmem = lambda x: pltpu.with_memory_space_constraint(x, pltpu.VMEM)
    kept = pltpu.VMEM((rows_dev, width), f32)
    dense = shape((rows_dev, width), f32)
    parcel = shape((room + META, width), jnp.int16)
    params = lambda mib: pltpu.CompilerParams(vmem_limit_bytes=mib * MIB)
    effort = lambda flops, moved: pl.CostEstimate(flops=flops, bytes_accessed=moved, transcendentals=0)
    near, far = peers // 2, peers - peers // 2
    line = pltpu.VMEM((1, tok_dev), jnp.int32)
    *packed_far, rel, rank, wide, table_kept, first_kept = pl.pallas_call(
        functools.partial(pack_far_kernel, peers, rows_dev, room),
        out_shape=(parcel,) * far
        + (line, line, pltpu.VMEM((tok_dev, 2 * width), jnp.bfloat16), kept, kept),
        in_specs=[hbm] * 4,
        out_specs=(vmem,) * (far + 5),
        scratch_shapes=[
            pltpu.VMEM((1, tok_dev), jnp.int32),
            pltpu.VMEM((tok_dev, width), jnp.bfloat16),
            pltpu.SemaphoreType.DMA((4,)),
        ],
        compiler_params=params(24),
        name="pack_far",
    )(*[in_hbm(x) for x in (ids.reshape(1, tok_dev), grads, table, first_moment)])
    got = [None] * peers
    for hop in range(peers - 1, near - 1, -1):
        got[hop] = lax.ppermute(packed_far[hop - near], "dp", hop_pairs(hop, peers))
    *packed_near, second_kept = pl.pallas_call(
        functools.partial(pack_near_kernel, peers, rows_dev, room),
        out_shape=(parcel,) * near + (kept,),
        in_specs=[vmem, vmem, vmem, hbm],
        out_specs=(vmem,) * (near + 1),
        scratch_shapes=[pltpu.SemaphoreType.DMA],
        compiler_params=params(24),
        cost_estimate=effort(4 * tok_dev * near * room * width, 16 * rows_dev * width),
        name="pack_near",
    )(in_vmem(rel), in_vmem(rank), in_vmem(wide), in_hbm(second_moment))
    got[0] = packed_near[0]
    for hop in range(near - 1, 0, -1):
        got[hop] = lax.ppermute(packed_near[hop], "dp", hop_pairs(hop, peers))
    longer = pltpu.VMEM((rows_dev + 8, width), f32)

    half, most = far // 2, 3 * far // 4
    hops = list(range(peers - 1, 0, -1))
    rounds = [[0, *hops[:half]], [*hops[half:most], *hops[far:]], hops[most:far]]
    grad_rows = part = None
    for n, members in enumerate(rounds):
        opens, ends = n == 0, n == len(rounds) - 1
        group = len(members)
        grad_rows, part = pl.pallas_call(
            functools.partial(join_kernel, group, room, opens, ends),
            out_shape=(longer, shape((everyone, 1, width) if ends else (8, LANES), f32)),
            in_specs=[vmem] * (group if opens else group + 2),
            out_specs=(vmem,) * 2,
            input_output_aliases={} if opens else {group: 0},
            scratch_shapes=[
                pltpu.VMEM((group * room, 2 * width), jnp.bfloat16),
                pltpu.VMEM((group * room, width), f32),
                pltpu.VMEM((group * room, width), f32),
                pltpu.VMEM((group * strips, LANES), jnp.int32),
                pltpu.SMEM((group * strips, LANES), jnp.int32),
                pltpu.SemaphoreType.DMA,
            ],
            compiler_params=params(16),
            cost_estimate=effort(width, width),
            name="join_rows_%d" % n,
        )(*[got[hop] for hop in members], *(() if opens else (in_vmem(grad_rows), part)))
    parts = lax.all_to_all(part, ("dp", "mp"), split_axis=0, concat_axis=0, tiled=True)
    limit = math.sqrt(tok_dev * everyone * width)
    step = math.gcd(1024, rows_dev)
    return pl.pallas_call(
        functools.partial(update_kernel, limit, step),
        out_shape=(dense,) * 3,
        in_specs=[vmem] * 5,
        out_specs=(hbm,) * 3,
        scratch_shapes=[pltpu.VMEM((rows_dev, width), f32)] * 3 + [pltpu.SemaphoreType.DMA((3, rows_dev // step))],
        compiler_params=params(20),
        name="update_rows",
    )(parts, *[in_vmem(x) for x in (grad_rows, table_kept, first_kept, second_kept)])


def solution(mesh):
    in_specs = (P("dp", "mp"), P("dp", "mp"), P("dp", "mp"), P("dp", "mp"), P("dp"))
    out_specs = (P("dp", "mp"), P("dp", "mp"), P("dp", "mp"))
    return jax.shard_map(body, mesh=mesh, in_specs=in_specs, out_specs=out_specs, check_vma=False)
```

```python
import functools
import math

import jax
import jax.numpy as jnp
from jax import lax
from jax.experimental import pallas as pl
from jax.experimental.pallas import tpu as pltpu
from jax.sharding import PartitionSpec as P

beta_first = 0.9
beta_second = 0.999
learn_rate = 0.01
decay_rate = 0.1
adam_eps = 1e-08
first_fix = 0.9999734386
second_fix = 0.0952078529

LANES = 128
META = 16
TOP = 32767.0
MIB = 2**20


def strip_rows(room):
    return -(-room // LANES)


def relative(me, owner, peers):
    return owner ^ me if peers & (peers - 1) == 0 else lax.rem(owner - me + peers, peers)


def hop_pairs(hop, peers):
    return [(i, i ^ hop if peers & (peers - 1) == 0 else (i + hop) % peers) for i in range(peers)]


def one_hot(keys, count):
    tall = 16 if count % 16 == 0 else count
    place = lax.broadcasted_iota(jnp.int32, (tall, keys.shape[1]), 0).astype(jnp.int16)
    keys = jnp.broadcast_to(keys, (tall, keys.shape[1])).astype(jnp.int16)
    one, zero = jnp.ones(keys.shape, jnp.bfloat16), jnp.zeros(keys.shape, jnp.bfloat16)
    return jnp.concatenate([jnp.where(place == keys - k, one, zero) for k in range(0, count, tall)], axis=0)


def rank_tables(group, per_owner):
    bf16 = jnp.bfloat16
    row = lax.broadcasted_iota(jnp.int32, (LANES, LANES), 0)
    column = lax.broadcasted_iota(jnp.int32, (LANES, LANES), 1)
    before = jnp.where(column < row, 1.0, 0.0).astype(bf16)
    ones = jnp.ones((LANES, LANES), bf16)
    source = lax.broadcasted_iota(jnp.int32, (per_owner, per_owner), 0)
    target = lax.broadcasted_iota(jnp.int32, (per_owner, per_owner), 1)
    ahead = jnp.where(source < target, 1.0, 0.0)
    blank = jnp.zeros((per_owner, per_owner), jnp.float32)
    rows = [jnp.concatenate([ahead if k == o else blank for k in range(group)], axis=1) for o in range(group)]
    return before, ones, jnp.concatenate(rows, axis=0).astype(bf16)


def slot_ranks(rel, tables):
    f32, bf16 = jnp.float32, jnp.bfloat16
    before, ones, ahead = tables
    high_hot = one_hot(rel >> 7, ahead.shape[0])
    low_hot = one_hot(rel & (LANES - 1), LANES)
    counts = lax.dot_general(low_hot, high_hot, (((1,), (1,)), ((), ())), preferred_element_type=f32)
    present = jnp.where(counts > 0.0, 1.0, 0.0).astype(bf16)
    within = jnp.dot(before, present, preferred_element_type=f32)
    totals = jnp.dot(ones, present, preferred_element_type=f32).astype(bf16)
    ranks = within + jnp.dot(totals, ahead, preferred_element_type=f32)
    by_low = jnp.dot(ranks.astype(bf16), high_hot, preferred_element_type=f32)
    return jnp.sum(by_low * low_hot.astype(f32), axis=0, keepdims=True).astype(jnp.int32)


def pack_group(rel, rank, wide, first, outs, rows_dev, room):
    f32 = jnp.float32
    group = len(outs)
    strips = strip_rows(room)
    lane = lax.broadcasted_iota(jnp.int32, (room, LANES), 1)
    meta = jnp.zeros((room, LANES), f32)
    for o in range(group):
        inside = jnp.logical_and(rel >= (first + o) * rows_dev, rel < (first + o + 1) * rows_dev)
        match = one_hot(jnp.where(inside, rank, -1), room)
        summed = jnp.dot(match, wide, preferred_element_type=f32)
        sums = summed[:, :LANES]
        digit_high = summed[:, LANES : LANES + 1]
        digit_low = summed[:, LANES + 1 : LANES + 2]
        number = summed[:, LANES + 2 : LANES + 3]
        mark = jnp.where(
            number > 0.0,
            jnp.floor((digit_high * LANES + digit_low) / jnp.maximum(number, 1.0) + 0.5),
            float(rows_dev),
        )
        largest = jnp.max(jnp.abs(sums), axis=1, keepdims=True)
        power = jnp.ceil(jnp.log2(jnp.maximum(largest, 1e-30) * (1.0 / TOP)))
        code = jnp.clip(jnp.round(sums * jnp.exp2(-power)), -TOP, TOP)
        outs[o][:room, :] = code.astype(jnp.int32).astype(jnp.int16)
        meta = jnp.where(lane == 2 * o, mark, jnp.where(lane == 2 * o + 1, power, meta))
    flat = meta.T.astype(jnp.int32)
    for o in range(group):
        rows = []
        for k in range(2):
            for c in range(strips):
                piece = flat[2 * o + k : 2 * o + k + 1, c * LANES : min((c + 1) * LANES, room)]
                if piece.shape[1] < LANES:
                    piece = jnp.concatenate([piece, jnp.zeros((1, LANES - piece.shape[1]), jnp.int32)], axis=1)
                rows.append(piece)
        rows.append(jnp.zeros((META - len(rows), LANES), jnp.int32))
        outs[o][room:, :] = jnp.concatenate(rows, axis=0).astype(jnp.int16)


def low_part(ids, size):
    return ids & (size - 1) if size & (size - 1) == 0 else lax.rem(ids, size)


def relative_rows(ids, peers, rows_dev):
    me = lax.axis_index("dp")
    if rows_dev & (rows_dev - 1) == 0 and peers & (peers - 1) == 0:
        return ids ^ (me * rows_dev)
    owner = ids // rows_dev
    return relative(me, owner, peers) * rows_dev + (ids - owner * rows_dev)


def pack_far_kernel(peers, rows_dev, room, ids_hbm, grads_hbm, table_hbm, *refs):
    far = peers - peers // 2
    outs, refs = refs[:far], refs[far:]
    rel_ref, rank_ref, wide_ref, table_ref, ids_ref, grads_ref, sems = refs
    pairs = ((ids_hbm, ids_ref), (grads_hbm, grads_ref), (table_hbm, table_ref))
    copies = [pltpu.make_async_copy(a, b, sems.at[n]) for n, (a, b) in enumerate(pairs)]
    copies[0].start()
    copies[1].start()
    tables = rank_tables(peers, rows_dev // LANES)
    copies[0].wait()
    for copy in copies[2:]:
        copy.start()
    rel = relative_rows(ids_ref[...], peers, rows_dev)
    tok = rel.shape[1]
    rank = slot_ranks(rel, tables)
    rel_ref[...] = rel
    rank_ref[...] = rank
    sub = lax.broadcasted_iota(jnp.int32, (8, tok), 0)
    high = low_part(rel, rows_dev) >> 7
    low = rel & (LANES - 1)
    digits = jnp.where(sub == 0, high, jnp.where(sub == 1, low, jnp.where(sub == 2, 1, 0))).astype(jnp.float32)
    aux = []
    for c in range(tok // LANES):
        tile = digits[:, c * LANES : (c + 1) * LANES]
        tile = jnp.concatenate([tile, jnp.zeros((LANES - 8, LANES), jnp.float32)], axis=0)
        aux.append(tile.T)
    copies[1].wait()
    wide = jnp.concatenate([grads_ref[...], jnp.concatenate(aux, axis=0).astype(jnp.bfloat16)], axis=1)
    wide_ref[...] = wide
    pack_group(rel, rank, wide, peers // 2, outs, rows_dev, room)
    for copy in copies[2:]:
        copy.wait()


def pack_near_kernel(peers, rows_dev, room, rel_ref, rank_ref, wide_ref, second_hbm, *refs):
    outs, (second_ref, sem) = refs[: peers // 2], refs[peers // 2 :]
    copy = pltpu.make_async_copy(second_hbm, second_ref, sem)
    copy.start()
    pack_group(rel_ref[...], rank_ref[...], wide_ref[...], 0, outs, rows_dev, room)
    copy.wait()


def open_blocks(got, room, marks_buf, slots, sem, wide):
    strips = strip_rows(room)
    f32, bf16 = jnp.float32, jnp.bfloat16
    lines = len(got) * strips
    strip = min(room, LANES)
    mark_rows, power_rows = [], []
    for ref in got:
        meta = ref[room:, :].astype(jnp.int32)
        mark_rows.append(meta[0:strips])
        power_rows.append(meta[strips : 2 * strips])
    marks = jnp.concatenate(mark_rows, axis=0)
    marks_buf[...] = marks
    copy = pltpu.make_async_copy(marks_buf, slots, sem)
    copy.start()
    fill = jnp.zeros((LANES - 2 * lines, LANES), jnp.int32)
    both = jnp.concatenate([marks] + power_rows + [fill], axis=0).astype(f32)
    columns = both.T
    mark_columns = columns.astype(jnp.int32)
    scale_columns = jnp.exp2(columns)
    mark_line = jnp.concatenate([marks[k : k + 1, :strip] for k in range(lines)], axis=1)
    power_line = jnp.concatenate([both[lines + k : lines + k + 1, :strip] for k in range(lines)], axis=1)
    scale_line = jnp.exp2(power_line)
    for s, ref in enumerate(got):
        code = ref[:room, :].astype(jnp.int32)
        upper = (code + 128) >> 8
        lower = code - upper * 256
        halves = jnp.concatenate([upper.astype(f32), lower.astype(f32)], axis=1)
        wide[s * room : (s + 1) * room, :] = halves.astype(bf16)
    return copy, lines, strip, mark_line, scale_line, mark_columns, scale_columns


def block_sums(block, strip, mark_line, scale_line, mark_columns, wide):
    same = [
        jnp.where(mark_columns[:strip, k : k + 1] == mark_line, scale_line, 0.0).astype(jnp.bfloat16) for k in block
    ]
    sums = jnp.dot(jnp.concatenate(same, axis=0), wide[...], preferred_element_type=jnp.float32)
    return sums[:, :LANES] * 256.0 + sums[:, LANES:]


def own_rows(k, strip, lines, scale_columns, wide):
    own = wide[k * strip : (k + 1) * strip, :].astype(jnp.float32)
    return (own[:, :LANES] * 256.0 + own[:, LANES:]) * scale_columns[:strip, lines + k : lines + k + 1]


def fold(product):
    return jnp.sum(product.reshape(product.shape[0] // 8, 8, LANES), axis=0)


def line_blocks(lines, strip):
    per_block = max(1, 256 // strip)
    return [range(k, min(k + per_block, lines)) for k in range(0, lines, per_block)]


def join_kernel(group, room, opens, ends, *refs):
    got, refs = refs[:group], refs[group:]
    if not opens:
        (_, sum_ref), refs = refs[:2], refs[2:]
    middle = not opens and not ends
    if middle:
        state_hbm, grad_ref, part_ref, state_ref, *refs, state_sem = refs
        state_copy = pltpu.make_async_copy(state_hbm, state_ref, state_sem)
        state_copy.start()
    else:
        grad_ref, part_ref, *refs = refs
    wide, sums_buf, before_buf, marks_buf, slots, sem = refs
    if opens:
        grad_ref[...] = jnp.zeros_like(grad_ref)
    copy, lines, strip, mark_line, scale_line, mark_columns, scale_columns = open_blocks(
        got, room, marks_buf, slots, sem, wide
    )
    total = jnp.zeros((8, LANES), jnp.float32) if opens else sum_ref[...]
    if not opens:
        copy.wait()
        for k in range(lines):
            for r in range(strip):
                before_buf[k * strip + r : k * strip + r + 1, :] = grad_ref[pl.ds(slots[k, r], 1), :]
    for block in line_blocks(lines, strip):
        sums = block_sums(block, strip, mark_line, scale_line, mark_columns, wide)
        for n, k in enumerate(block):
            here = slice(k * strip, (k + 1) * strip)
            after = sums[n * strip : (n + 1) * strip]
            twice = after
            if not opens:
                before = before_buf[here, :]
                after = before + after
                twice = before + after
            sums_buf[here, :] = after
            total = total + fold(own_rows(k, strip, lines, scale_columns, wide) * twice)
        if opens and block[0] == 0:
            copy.wait()
        for k in block:
            for r in range(strip):
                grad_ref[pl.ds(slots[k, r], 1), :] = sums_buf[k * strip + r : k * strip + r + 1, :]
    if ends:
        total = jnp.sum(total, axis=0, keepdims=True)
        total = jnp.sum(total, axis=1, keepdims=True)
        part_ref[...] = jnp.broadcast_to(total[None], part_ref.shape)
    else:
        part_ref[...] = total
    if middle:
        state_copy.wait()


def update_kernel(limit, step, parts_ref, grad_ref, table_ref, first_ref, second_ref, table_out, first_out, second_out,
                  table_buf, first_buf, second_buf, sems):
    total = jnp.sum(parts_ref[...], axis=0)
    scale = limit / jnp.maximum(jnp.sqrt(total), limit)
    rows = table_ref.shape[0]
    copies = []
    for n in range(rows // step):
        part = pl.ds(n * step, step)
        clipped = scale * grad_ref[part, :]
        new_first = beta_first * first_ref[part, :] + (1.0 - beta_first) * clipped
        first_buf[part, :] = new_first
        new_second = beta_second * second_ref[part, :] + (1.0 - beta_second) * clipped * clipped
        second_buf[part, :] = new_second
        change = (new_first * (learn_rate / first_fix)) / (jnp.sqrt(new_second * (1.0 / second_fix)) + adam_eps)
        table_buf[part, :] = table_ref[part, :] * (1.0 - learn_rate * decay_rate) - change
        for k, (a, b) in enumerate(((first_buf, first_out), (second_buf, second_out), (table_buf, table_out))):
            copy = pltpu.make_async_copy(a.at[part], b.at[part], sems.at[k, n])
            copy.start()
            copies.append(copy)
    for copy in copies:
        copy.wait()


def body(table, first_moment, second_moment, grads, ids):
    peers = lax.axis_size("dp")
    everyone = peers * lax.axis_size("mp")
    rows_dev, width = table.shape
    tok_dev = grads.shape[0]
    room = tok_dev // peers
    strips = strip_rows(room)
    f32 = jnp.float32
    shape = jax.ShapeDtypeStruct
    vmem = pl.BlockSpec(memory_space=pltpu.VMEM)
    hbm = pl.BlockSpec(memory_space=pltpu.HBM)
    in_hbm = lambda x: pltpu.with_memory_space_constraint(x, pltpu.HBM)
    in_vmem = lambda x: pltpu.with_memory_space_constraint(x, pltpu.VMEM)
    kept = pltpu.VMEM((rows_dev, width), f32)
    dense = shape((rows_dev, width), f32)
    parcel = shape((room + META, width), jnp.int16)
    params = lambda mib: pltpu.CompilerParams(vmem_limit_bytes=mib * MIB)
    effort = lambda flops, moved: pl.CostEstimate(flops=flops, bytes_accessed=moved, transcendentals=0)
    near, far = peers // 2, peers - peers // 2
    line = pltpu.VMEM((1, tok_dev), jnp.int32)
    *packed_far, rel, rank, wide, table_kept = pl.pallas_call(
        functools.partial(pack_far_kernel, peers, rows_dev, room),
        out_shape=(parcel,) * far
        + (line, line, pltpu.VMEM((tok_dev, 2 * width), jnp.bfloat16), kept),
        in_specs=[hbm] * 3,
        out_specs=(vmem,) * (far + 4),
        scratch_shapes=[
            pltpu.VMEM((1, tok_dev), jnp.int32),
            pltpu.VMEM((tok_dev, width), jnp.bfloat16),
            pltpu.SemaphoreType.DMA((3,)),
        ],
        compiler_params=params(24),
        name="pack_far",
    )(*[in_hbm(x) for x in (ids.reshape(1, tok_dev), grads, table)])
    got = [None] * peers
    for hop in range(peers - 1, near - 1, -1):
        got[hop] = lax.ppermute(packed_far[hop - near], "dp", hop_pairs(hop, peers))
    *packed_near, second_kept = pl.pallas_call(
        functools.partial(pack_near_kernel, peers, rows_dev, room),
        out_shape=(parcel,) * near + (kept,),
        in_specs=[vmem, vmem, vmem, hbm],
        out_specs=(vmem,) * (near + 1),
        scratch_shapes=[pltpu.SemaphoreType.DMA],
        compiler_params=params(24),
        cost_estimate=effort(4 * tok_dev * near * room * width, 16 * rows_dev * width),
        name="pack_near",
    )(in_vmem(rel), in_vmem(rank), in_vmem(wide), in_hbm(second_moment))
    got[0] = packed_near[0]
    for hop in range(near - 1, 0, -1):
        got[hop] = lax.ppermute(packed_near[hop], "dp", hop_pairs(hop, peers))
    longer = pltpu.VMEM((rows_dev + 8, width), f32)

    half, most = far // 2, 3 * far // 4
    hops = list(range(peers - 1, 0, -1))
    rounds = [[0, *hops[:half]], [*hops[half:most], *hops[far:]], hops[most:far]]
    grad_rows = part = None
    for n, members in enumerate(rounds):
        opens, ends = n == 0, n == len(rounds) - 1
        middle = not opens and not ends
        group = len(members)
        operands = [got[hop] for hop in members]
        if not opens:
            operands += [in_vmem(grad_rows), part]
        if middle:
            operands.append(in_hbm(first_moment))
        grad_rows, part, *state = pl.pallas_call(
            functools.partial(join_kernel, group, room, opens, ends),
            out_shape=(longer, shape((everyone, 1, width) if ends else (8, LANES), f32)) + (kept,) * middle,
            in_specs=[vmem] * (len(operands) - middle) + [hbm] * middle,
            out_specs=(vmem,) * (2 + middle),
            input_output_aliases={} if opens else {group: 0},
            scratch_shapes=[
                pltpu.VMEM((group * room, 2 * width), jnp.bfloat16),
                pltpu.VMEM((group * room, width), f32),
                pltpu.VMEM((group * room, width), f32),
                pltpu.VMEM((group * strips, LANES), jnp.int32),
                pltpu.SMEM((group * strips, LANES), jnp.int32),
                pltpu.SemaphoreType.DMA,
            ]
            + [pltpu.SemaphoreType.DMA] * middle,
            compiler_params=params(16),
            cost_estimate=effort(width, width),
            name="join_rows_%d" % n,
        )(*operands)
        if middle:
            (first_kept,) = state
    parts = lax.all_to_all(part, ("dp", "mp"), split_axis=0, concat_axis=0, tiled=True)
    limit = math.sqrt(tok_dev * everyone * width)
    step = math.gcd(1024, rows_dev)
    return pl.pallas_call(
        functools.partial(update_kernel, limit, step),
        out_shape=(dense,) * 3,
        in_specs=[vmem] * 5,
        out_specs=(hbm,) * 3,
        scratch_shapes=[pltpu.VMEM((rows_dev, width), f32)] * 3 + [pltpu.SemaphoreType.DMA((3, rows_dev // step))],
        compiler_params=params(20),
        name="update_rows",
    )(parts, *[in_vmem(x) for x in (grad_rows, table_kept, first_kept, second_kept)])


def solution(mesh):
    in_specs = (P("dp", "mp"), P("dp", "mp"), P("dp", "mp"), P("dp", "mp"), P("dp"))
    out_specs = (P("dp", "mp"), P("dp", "mp"), P("dp", "mp"))
    return jax.shard_map(body, mesh=mesh, in_specs=in_specs, out_specs=out_specs, check_vma=False)
```

```python
import functools
import math

import jax
import jax.numpy as jnp
from jax import lax
from jax.experimental import pallas as pl
from jax.experimental.pallas import tpu as pltpu
from jax.sharding import PartitionSpec as P

beta_first = 0.9
beta_second = 0.999
learn_rate = 0.01
decay_rate = 0.1
adam_eps = 1e-08
first_fix = 0.9999734386
second_fix = 0.0952078529

LANES = 128
META = 16
TOP = 32767.0
MIB = 2**20


def strip_rows(room):
    return -(-room // LANES)


def relative(me, owner, peers):
    return owner ^ me if peers & (peers - 1) == 0 else lax.rem(owner - me + peers, peers)


def hop_pairs(hop, peers):
    return [(i, i ^ hop if peers & (peers - 1) == 0 else (i + hop) % peers) for i in range(peers)]


def one_hot(keys, count):
    tall = 16 if count % 16 == 0 else count
    place = lax.broadcasted_iota(jnp.int32, (tall, keys.shape[1]), 0).astype(jnp.int16)
    keys = jnp.broadcast_to(keys, (tall, keys.shape[1])).astype(jnp.int16)
    one, zero = jnp.ones(keys.shape, jnp.bfloat16), jnp.zeros(keys.shape, jnp.bfloat16)
    return jnp.concatenate([jnp.where(place == keys - k, one, zero) for k in range(0, count, tall)], axis=0)


def rank_tables(group, per_owner):
    bf16 = jnp.bfloat16
    row = lax.broadcasted_iota(jnp.int32, (LANES, LANES), 0)
    column = lax.broadcasted_iota(jnp.int32, (LANES, LANES), 1)
    before = jnp.where(column < row, 1.0, 0.0).astype(bf16)
    ones = jnp.ones((LANES, LANES), bf16)
    source = lax.broadcasted_iota(jnp.int32, (per_owner, per_owner), 0)
    target = lax.broadcasted_iota(jnp.int32, (per_owner, per_owner), 1)
    ahead = jnp.where(source < target, 1.0, 0.0)
    blank = jnp.zeros((per_owner, per_owner), jnp.float32)
    rows = [jnp.concatenate([ahead if k == o else blank for k in range(group)], axis=1) for o in range(group)]
    return before, ones, jnp.concatenate(rows, axis=0).astype(bf16)


def slot_ranks(rel, tables):
    f32, bf16 = jnp.float32, jnp.bfloat16
    before, ones, ahead = tables
    high_hot = one_hot(rel >> 7, ahead.shape[0])
    low_hot = one_hot(rel & (LANES - 1), LANES)
    counts = lax.dot_general(low_hot, high_hot, (((1,), (1,)), ((), ())), preferred_element_type=f32)
    present = jnp.where(counts > 0.0, 1.0, 0.0).astype(bf16)
    within = jnp.dot(before, present, preferred_element_type=f32)
    totals = jnp.dot(ones, present, preferred_element_type=f32).astype(bf16)
    ranks = within + jnp.dot(totals, ahead, preferred_element_type=f32)
    by_low = jnp.dot(ranks.astype(bf16), high_hot, preferred_element_type=f32)
    return jnp.sum(by_low * low_hot.astype(f32), axis=0, keepdims=True).astype(jnp.int32)


def pack_group(rel, rank, wide, first, outs, rows_dev, room):
    f32 = jnp.float32
    group = len(outs)
    strips = strip_rows(room)
    lane = lax.broadcasted_iota(jnp.int32, (room, LANES), 1)
    meta = jnp.zeros((room, LANES), f32)
    for o in range(group):
        inside = jnp.logical_and(rel >= (first + o) * rows_dev, rel < (first + o + 1) * rows_dev)
        match = one_hot(jnp.where(inside, rank, -1), room)
        summed = jnp.dot(match, wide, preferred_element_type=f32)
        sums = summed[:, :LANES]
        digit_high = summed[:, LANES : LANES + 1]
        digit_low = summed[:, LANES + 1 : LANES + 2]
        number = summed[:, LANES + 2 : LANES + 3]
        mark = jnp.where(
            number > 0.0,
            jnp.floor((digit_high * LANES + digit_low) / jnp.maximum(number, 1.0) + 0.5),
            float(rows_dev),
        )
        largest = jnp.max(jnp.abs(sums), axis=1, keepdims=True)
        power = jnp.ceil(jnp.log2(jnp.maximum(largest, 1e-30) * (1.0 / TOP)))
        code = jnp.clip(jnp.round(sums * jnp.exp2(-power)), -TOP, TOP)
        outs[o][:room, :] = code.astype(jnp.int32).astype(jnp.int16)
        meta = jnp.where(lane == 2 * o, mark, jnp.where(lane == 2 * o + 1, power, meta))
    flat = meta.T.astype(jnp.int32)
    for o in range(group):
        rows = []
        for k in range(2):
            for c in range(strips):
                piece = flat[2 * o + k : 2 * o + k + 1, c * LANES : min((c + 1) * LANES, room)]
                if piece.shape[1] < LANES:
                    piece = jnp.concatenate([piece, jnp.zeros((1, LANES - piece.shape[1]), jnp.int32)], axis=1)
                rows.append(piece)
        rows.append(jnp.zeros((META - len(rows), LANES), jnp.int32))
        outs[o][room:, :] = jnp.concatenate(rows, axis=0).astype(jnp.int16)


def low_part(ids, size):
    return ids & (size - 1) if size & (size - 1) == 0 else lax.rem(ids, size)


def relative_rows(ids, peers, rows_dev):
    me = lax.axis_index("dp")
    if rows_dev & (rows_dev - 1) == 0 and peers & (peers - 1) == 0:
        return ids ^ (me * rows_dev)
    owner = ids // rows_dev
    return relative(me, owner, peers) * rows_dev + (ids - owner * rows_dev)


def pack_far_kernel(peers, rows_dev, room, ids_hbm, grads_hbm, table_hbm, *refs):
    far = peers - peers // 2
    outs, refs = refs[:far], refs[far:]
    rel_ref, rank_ref, wide_ref, table_ref, ids_ref, grads_ref, sems = refs
    pairs = ((ids_hbm, ids_ref), (grads_hbm, grads_ref), (table_hbm, table_ref))
    copies = [pltpu.make_async_copy(a, b, sems.at[n]) for n, (a, b) in enumerate(pairs)]
    copies[0].start()
    copies[1].start()
    tables = rank_tables(peers, rows_dev // LANES)
    copies[0].wait()
    for copy in copies[2:]:
        copy.start()
    rel = relative_rows(ids_ref[...], peers, rows_dev)
    tok = rel.shape[1]
    rank = slot_ranks(rel, tables)
    rel_ref[...] = rel
    rank_ref[...] = rank
    sub = lax.broadcasted_iota(jnp.int32, (8, tok), 0)
    high = low_part(rel, rows_dev) >> 7
    low = rel & (LANES - 1)
    digits = jnp.where(sub == 0, high, jnp.where(sub == 1, low, jnp.where(sub == 2, 1, 0))).astype(jnp.float32)
    aux = []
    for c in range(tok // LANES):
        tile = digits[:, c * LANES : (c + 1) * LANES]
        tile = jnp.concatenate([tile, jnp.zeros((LANES - 8, LANES), jnp.float32)], axis=0)
        aux.append(tile.T)
    copies[1].wait()
    wide = jnp.concatenate([grads_ref[...], jnp.concatenate(aux, axis=0).astype(jnp.bfloat16)], axis=1)
    wide_ref[...] = wide
    pack_group(rel, rank, wide, peers // 2, outs, rows_dev, room)
    for copy in copies[2:]:
        copy.wait()


def pack_near_kernel(peers, rows_dev, room, rel_ref, rank_ref, wide_ref, second_hbm, *refs):
    outs, (second_ref, sem) = refs[: peers // 2], refs[peers // 2 :]
    copy = pltpu.make_async_copy(second_hbm, second_ref, sem)
    copy.start()
    pack_group(rel_ref[...], rank_ref[...], wide_ref[...], 0, outs, rows_dev, room)
    copy.wait()


def open_blocks(got, room, marks_buf, slots, sem, wide):
    strips = strip_rows(room)
    f32, bf16 = jnp.float32, jnp.bfloat16
    lines = len(got) * strips
    strip = min(room, LANES)
    mark_rows, power_rows = [], []
    for ref in got:
        meta = ref[room:, :].astype(jnp.int32)
        mark_rows.append(meta[0:strips])
        power_rows.append(meta[strips : 2 * strips])
    marks = jnp.concatenate(mark_rows, axis=0)
    marks_buf[...] = marks
    copy = pltpu.make_async_copy(marks_buf, slots, sem)
    copy.start()
    fill = jnp.zeros((LANES - 2 * lines, LANES), jnp.int32)
    both = jnp.concatenate([marks] + power_rows + [fill], axis=0).astype(f32)
    columns = both.T
    mark_columns = columns.astype(jnp.int32)
    scale_columns = jnp.exp2(columns)
    mark_line = jnp.concatenate([marks[k : k + 1, :strip] for k in range(lines)], axis=1)
    power_line = jnp.concatenate([both[lines + k : lines + k + 1, :strip] for k in range(lines)], axis=1)
    scale_line = jnp.exp2(power_line)
    for s, ref in enumerate(got):
        code = ref[:room, :].astype(jnp.int32)
        upper = (code + 128) >> 8
        lower = code - upper * 256
        halves = jnp.concatenate([upper.astype(f32), lower.astype(f32)], axis=1)
        wide[s * room : (s + 1) * room, :] = halves.astype(bf16)
    return copy, lines, strip, mark_line, scale_line, mark_columns, scale_columns


def block_sums(block, strip, mark_line, scale_line, mark_columns, wide):
    same = [
        jnp.where(mark_columns[:strip, k : k + 1] == mark_line, scale_line, 0.0).astype(jnp.bfloat16) for k in block
    ]
    sums = jnp.dot(jnp.concatenate(same, axis=0), wide[...], preferred_element_type=jnp.float32)
    return sums[:, :LANES] * 256.0 + sums[:, LANES:]


def own_rows(k, strip, lines, scale_columns, wide):
    own = wide[k * strip : (k + 1) * strip, :].astype(jnp.float32)
    return (own[:, :LANES] * 256.0 + own[:, LANES:]) * scale_columns[:strip, lines + k : lines + k + 1]


def fold(product):
    return jnp.sum(product.reshape(product.shape[0] // 8, 8, LANES), axis=0)


def line_blocks(lines, strip):
    per_block = max(1, 256 // strip)
    return [range(k, min(k + per_block, lines)) for k in range(0, lines, per_block)]


def join_kernel(group, room, opens, ends, *refs):
    got, refs = refs[:group], refs[group:]
    if not opens:
        (_, sum_ref), refs = refs[:2], refs[2:]
    middle = not opens and not ends
    if middle:
        state_hbm, grad_ref, part_ref, state_ref, *refs, state_sem = refs
        state_copy = pltpu.make_async_copy(state_hbm, state_ref, state_sem)
        state_copy.start()
    else:
        grad_ref, part_ref, *refs = refs
    wide, sums_buf, before_buf, marks_buf, slots, sem = refs
    if opens:
        grad_ref[...] = jnp.zeros_like(grad_ref)
    copy, lines, strip, mark_line, scale_line, mark_columns, scale_columns = open_blocks(
        got, room, marks_buf, slots, sem, wide
    )
    total = jnp.zeros((8, LANES), jnp.float32) if opens else sum_ref[...]
    if not opens:
        copy.wait()
        for k in range(lines):
            for r in range(strip):
                before_buf[k * strip + r : k * strip + r + 1, :] = grad_ref[pl.ds(slots[k, r], 1), :]
    for block in line_blocks(lines, strip):
        sums = block_sums(block, strip, mark_line, scale_line, mark_columns, wide)
        for n, k in enumerate(block):
            here = slice(k * strip, (k + 1) * strip)
            after = sums[n * strip : (n + 1) * strip]
            twice = after
            if not opens:
                before = before_buf[here, :]
                after = before + after
                twice = before + after
            sums_buf[here, :] = after
            total = total + fold(own_rows(k, strip, lines, scale_columns, wide) * twice)
        if opens and block[0] == 0:
            copy.wait()
        for k in block:
            for r in range(strip):
                grad_ref[pl.ds(slots[k, r], 1), :] = sums_buf[k * strip + r : k * strip + r + 1, :]
    if ends:
        total = jnp.sum(total, axis=0, keepdims=True)
        total = jnp.sum(total, axis=1, keepdims=True)
        part_ref[...] = jnp.broadcast_to(total[None], part_ref.shape)
    else:
        part_ref[...] = total
    if middle:
        state_copy.wait()


def update_kernel(limit, step, parts_ref, grad_ref, table_ref, first_ref, second_ref, table_out, first_out, second_out,
                  table_buf, first_buf, second_buf, sems):
    total = jnp.sum(parts_ref[...], axis=0)
    scale = limit / jnp.maximum(jnp.sqrt(total), limit)
    rows = table_ref.shape[0]
    copies = []
    for n in range(rows // step):
        part = pl.ds(n * step, step)
        clipped = scale * grad_ref[part, :]
        new_first = beta_first * first_ref[part, :] + (1.0 - beta_first) * clipped
        first_buf[part, :] = new_first
        new_second = beta_second * second_ref[part, :] + (1.0 - beta_second) * clipped * clipped
        second_buf[part, :] = new_second
        spread = new_second * (1.0 / second_fix)
        change = (new_first * (learn_rate / first_fix)) / (spread * lax.rsqrt(spread) + adam_eps)
        table_buf[part, :] = table_ref[part, :] * (1.0 - learn_rate * decay_rate) - change
        for k, (a, b) in enumerate(((first_buf, first_out), (second_buf, second_out), (table_buf, table_out))):
            copy = pltpu.make_async_copy(a.at[part], b.at[part], sems.at[k, n])
            copy.start()
            copies.append(copy)
    for copy in copies:
        copy.wait()


def body(table, first_moment, second_moment, grads, ids):
    peers = lax.axis_size("dp")
    everyone = peers * lax.axis_size("mp")
    rows_dev, width = table.shape
    tok_dev = grads.shape[0]
    room = tok_dev // peers
    strips = strip_rows(room)
    f32 = jnp.float32
    shape = jax.ShapeDtypeStruct
    vmem = pl.BlockSpec(memory_space=pltpu.VMEM)
    hbm = pl.BlockSpec(memory_space=pltpu.HBM)
    in_hbm = lambda x: pltpu.with_memory_space_constraint(x, pltpu.HBM)
    in_vmem = lambda x: pltpu.with_memory_space_constraint(x, pltpu.VMEM)
    kept = pltpu.VMEM((rows_dev, width), f32)
    dense = shape((rows_dev, width), f32)
    parcel = shape((room + META, width), jnp.int16)
    params = lambda mib: pltpu.CompilerParams(vmem_limit_bytes=mib * MIB)
    effort = lambda flops, moved: pl.CostEstimate(flops=flops, bytes_accessed=moved, transcendentals=0)
    near, far = peers // 2, peers - peers // 2
    line = pltpu.VMEM((1, tok_dev), jnp.int32)
    *packed_far, rel, rank, wide, table_kept = pl.pallas_call(
        functools.partial(pack_far_kernel, peers, rows_dev, room),
        out_shape=(parcel,) * far
        + (line, line, pltpu.VMEM((tok_dev, 2 * width), jnp.bfloat16), kept),
        in_specs=[hbm] * 3,
        out_specs=(vmem,) * (far + 4),
        scratch_shapes=[
            pltpu.VMEM((1, tok_dev), jnp.int32),
            pltpu.VMEM((tok_dev, width), jnp.bfloat16),
            pltpu.SemaphoreType.DMA((3,)),
        ],
        compiler_params=params(24),
        name="pack_far",
    )(*[in_hbm(x) for x in (ids.reshape(1, tok_dev), grads, table)])
    got = [None] * peers
    for hop in range(peers - 1, near - 1, -1):
        got[hop] = lax.ppermute(packed_far[hop - near], "dp", hop_pairs(hop, peers))
    *packed_near, second_kept = pl.pallas_call(
        functools.partial(pack_near_kernel, peers, rows_dev, room),
        out_shape=(parcel,) * near + (kept,),
        in_specs=[vmem, vmem, vmem, hbm],
        out_specs=(vmem,) * (near + 1),
        scratch_shapes=[pltpu.SemaphoreType.DMA],
        compiler_params=params(24),
        cost_estimate=effort(4 * tok_dev * near * room * width, 16 * rows_dev * width),
        name="pack_near",
    )(in_vmem(rel), in_vmem(rank), in_vmem(wide), in_hbm(second_moment))
    got[0] = packed_near[0]
    for hop in range(near - 1, 0, -1):
        got[hop] = lax.ppermute(packed_near[hop], "dp", hop_pairs(hop, peers))
    longer = pltpu.VMEM((rows_dev + 8, width), f32)

    half, most = far // 2, 3 * far // 4
    hops = [*range(near + far // 2, peers), *range(near + far // 2 - 1, 0, -1)]
    rounds = [[0, *hops[:half]], [*hops[half:most], *hops[far:]], hops[most:far]]
    grad_rows = part = None
    for n, members in enumerate(rounds):
        opens, ends = n == 0, n == len(rounds) - 1
        middle = not opens and not ends
        group = len(members)
        operands = [got[hop] for hop in members]
        if not opens:
            operands += [in_vmem(grad_rows), part]
        if middle:
            operands.append(in_hbm(first_moment))
        grad_rows, part, *state = pl.pallas_call(
            functools.partial(join_kernel, group, room, opens, ends),
            out_shape=(longer, shape((everyone, 1, width) if ends else (8, LANES), f32)) + (kept,) * middle,
            in_specs=[vmem] * (len(operands) - middle) + [hbm] * middle,
            out_specs=(vmem,) * (2 + middle),
            input_output_aliases={} if opens else {group: 0},
            scratch_shapes=[
                pltpu.VMEM((group * room, 2 * width), jnp.bfloat16),
                pltpu.VMEM((group * room, width), f32),
                pltpu.VMEM((group * room, width), f32),
                pltpu.VMEM((group * strips, LANES), jnp.int32),
                pltpu.SMEM((group * strips, LANES), jnp.int32),
                pltpu.SemaphoreType.DMA,
            ]
            + [pltpu.SemaphoreType.DMA] * middle,
            compiler_params=params(16),
            cost_estimate=effort(width, width),
            name="join_rows_%d" % n,
        )(*operands)
        if middle:
            (first_kept,) = state
    parts = lax.all_to_all(part, ("dp", "mp"), split_axis=0, concat_axis=0, tiled=True)
    limit = math.sqrt(tok_dev * everyone * width)
    step = math.gcd(1024, rows_dev)
    return pl.pallas_call(
        functools.partial(update_kernel, limit, step),
        out_shape=(dense,) * 3,
        in_specs=[vmem] * 5,
        out_specs=(hbm,) * 3,
        scratch_shapes=[pltpu.VMEM((rows_dev, width), f32)] * 3 + [pltpu.SemaphoreType.DMA((3, rows_dev // step))],
        compiler_params=params(20),
        name="update_rows",
    )(parts, *[in_vmem(x) for x in (grad_rows, table_kept, first_kept, second_kept)])


def solution(mesh):
    in_specs = (P("dp", "mp"), P("dp", "mp"), P("dp", "mp"), P("dp", "mp"), P("dp"))
    out_specs = (P("dp", "mp"), P("dp", "mp"), P("dp", "mp"))
    return jax.shard_map(body, mesh=mesh, in_specs=in_specs, out_specs=out_specs, check_vma=False)
```

```python
import functools
import math

import jax
import jax.numpy as jnp
from jax import lax
from jax.experimental import pallas as pl
from jax.experimental.pallas import tpu as pltpu
from jax.sharding import PartitionSpec as P

beta_first = 0.9
beta_second = 0.999
learn_rate = 0.01
decay_rate = 0.1
adam_eps = 1e-08
first_fix = 0.9999734386
second_fix = 0.0952078529

LANES = 128
META = 16
TOP = 32767.0
MIB = 2**20


def strip_rows(room):
    return -(-room // LANES)


def relative(me, owner, peers):
    return owner ^ me if peers & (peers - 1) == 0 else lax.rem(owner - me + peers, peers)


def hop_pairs(hop, peers):
    return [(i, i ^ hop if peers & (peers - 1) == 0 else (i + hop) % peers) for i in range(peers)]


def one_hot(keys, count):
    tall = 16 if count % 16 == 0 else count
    place = lax.broadcasted_iota(jnp.int32, (tall, keys.shape[1]), 0).astype(jnp.int16)
    keys = jnp.broadcast_to(keys, (tall, keys.shape[1])).astype(jnp.int16)
    one, zero = jnp.ones(keys.shape, jnp.bfloat16), jnp.zeros(keys.shape, jnp.bfloat16)
    return jnp.concatenate([jnp.where(place == keys - k, one, zero) for k in range(0, count, tall)], axis=0)


def rank_tables(group, per_owner):
    bf16 = jnp.bfloat16
    row = lax.broadcasted_iota(jnp.int32, (LANES, LANES), 0)
    column = lax.broadcasted_iota(jnp.int32, (LANES, LANES), 1)
    before = jnp.where(column < row, 1.0, 0.0).astype(bf16)
    ones = jnp.ones((LANES, LANES), bf16)
    source = lax.broadcasted_iota(jnp.int32, (per_owner, per_owner), 0)
    target = lax.broadcasted_iota(jnp.int32, (per_owner, per_owner), 1)
    ahead = jnp.where(source < target, 1.0, 0.0)
    blank = jnp.zeros((per_owner, per_owner), jnp.float32)
    rows = [jnp.concatenate([ahead if k == o else blank for k in range(group)], axis=1) for o in range(group)]
    return before, ones, jnp.concatenate(rows, axis=0).astype(bf16)


def slot_ranks(rel, tables):
    f32, bf16 = jnp.float32, jnp.bfloat16
    before, ones, ahead = tables
    high_hot = one_hot(rel >> 7, ahead.shape[0])
    low_hot = one_hot(rel & (LANES - 1), LANES)
    counts = lax.dot_general(low_hot, high_hot, (((1,), (1,)), ((), ())), preferred_element_type=f32)
    present = jnp.where(counts > 0.0, 1.0, 0.0).astype(bf16)
    within = jnp.dot(before, present, preferred_element_type=f32)
    totals = jnp.dot(ones, present, preferred_element_type=f32).astype(bf16)
    ranks = within + jnp.dot(totals, ahead, preferred_element_type=f32)
    by_low = jnp.dot(ranks.astype(bf16), high_hot, preferred_element_type=f32)
    return jnp.sum(by_low * low_hot.astype(f32), axis=0, keepdims=True).astype(jnp.int32)


def pack_group(rel, rank, wide, first, outs, rows_dev, room):
    f32 = jnp.float32
    group = len(outs)
    strips = strip_rows(room)
    lane = lax.broadcasted_iota(jnp.int32, (room, LANES), 1)
    meta = jnp.zeros((room, LANES), f32)
    for o in range(group):
        inside = jnp.logical_and(rel >= (first + o) * rows_dev, rel < (first + o + 1) * rows_dev)
        match = one_hot(jnp.where(inside, rank, -1), room)
        summed = jnp.dot(match, wide, preferred_element_type=f32)
        sums = summed[:, :LANES]
        digit_high = summed[:, LANES : LANES + 1]
        digit_low = summed[:, LANES + 1 : LANES + 2]
        number = summed[:, LANES + 2 : LANES + 3]
        mark = jnp.where(
            number > 0.0,
            jnp.floor((digit_high * LANES + digit_low) / jnp.maximum(number, 1.0) + 0.5),
            float(rows_dev),
        )
        largest = jnp.max(jnp.abs(sums), axis=1, keepdims=True)
        power = jnp.ceil(jnp.log2(jnp.maximum(largest, 1e-30) * (1.0 / TOP)))
        code = jnp.clip(jnp.round(sums * jnp.exp2(-power)), -TOP, TOP)
        outs[o][:room, :] = code.astype(jnp.int32).astype(jnp.int16)
        meta = jnp.where(lane == 2 * o, mark, jnp.where(lane == 2 * o + 1, power, meta))
    flat = meta.T.astype(jnp.int32)
    for o in range(group):
        rows = []
        for k in range(2):
            for c in range(strips):
                piece = flat[2 * o + k : 2 * o + k + 1, c * LANES : min((c + 1) * LANES, room)]
                if piece.shape[1] < LANES:
                    piece = jnp.concatenate([piece, jnp.zeros((1, LANES - piece.shape[1]), jnp.int32)], axis=1)
                rows.append(piece)
        rows.append(jnp.zeros((META - len(rows), LANES), jnp.int32))
        outs[o][room:, :] = jnp.concatenate(rows, axis=0).astype(jnp.int16)


def low_part(ids, size):
    return ids & (size - 1) if size & (size - 1) == 0 else lax.rem(ids, size)


def relative_rows(ids, peers, rows_dev):
    me = lax.axis_index("dp")
    if rows_dev & (rows_dev - 1) == 0 and peers & (peers - 1) == 0:
        return ids ^ (me * rows_dev)
    owner = ids // rows_dev
    return relative(me, owner, peers) * rows_dev + (ids - owner * rows_dev)


def pack_far_kernel(peers, rows_dev, room, ids_hbm, grads_hbm, table_hbm, *refs):
    far = peers - peers // 2
    outs, refs = refs[:far], refs[far:]
    rel_ref, rank_ref, wide_ref, table_ref, ids_ref, grads_ref, sems = refs
    pairs = ((ids_hbm, ids_ref), (grads_hbm, grads_ref), (table_hbm, table_ref))
    copies = [pltpu.make_async_copy(a, b, sems.at[n]) for n, (a, b) in enumerate(pairs)]
    copies[0].start()
    copies[1].start()
    tables = rank_tables(peers, rows_dev // LANES)
    copies[0].wait()
    for copy in copies[2:]:
        copy.start()
    rel = relative_rows(ids_ref[...], peers, rows_dev)
    tok = rel.shape[1]
    rank = slot_ranks(rel, tables)
    rel_ref[...] = rel
    rank_ref[...] = rank
    sub = lax.broadcasted_iota(jnp.int32, (8, tok), 0)
    high = low_part(rel, rows_dev) >> 7
    low = rel & (LANES - 1)
    digits = jnp.where(sub == 0, high, jnp.where(sub == 1, low, jnp.where(sub == 2, 1, 0))).astype(jnp.float32)
    aux = []
    for c in range(tok // LANES):
        tile = digits[:, c * LANES : (c + 1) * LANES]
        tile = jnp.concatenate([tile, jnp.zeros((LANES - 8, LANES), jnp.float32)], axis=0)
        aux.append(tile.T)
    copies[1].wait()
    wide = jnp.concatenate([grads_ref[...], jnp.concatenate(aux, axis=0).astype(jnp.bfloat16)], axis=1)
    wide_ref[...] = wide
    pack_group(rel, rank, wide, peers // 2, outs, rows_dev, room)
    for copy in copies[2:]:
        copy.wait()


def pack_near_kernel(peers, rows_dev, room, rel_ref, rank_ref, wide_ref, second_hbm, *refs):
    outs, (second_ref, sem) = refs[: peers // 2], refs[peers // 2 :]
    copy = pltpu.make_async_copy(second_hbm, second_ref, sem)
    copy.start()
    pack_group(rel_ref[...], rank_ref[...], wide_ref[...], 0, outs, rows_dev, room)
    copy.wait()


def open_blocks(got, room, marks_buf, slots, sem, wide):
    strips = strip_rows(room)
    f32, bf16 = jnp.float32, jnp.bfloat16
    lines = len(got) * strips
    strip = min(room, LANES)
    mark_rows, power_rows = [], []
    for ref in got:
        meta = ref[room:, :].astype(jnp.int32)
        mark_rows.append(meta[0:strips])
        power_rows.append(meta[strips : 2 * strips])
    marks = jnp.concatenate(mark_rows, axis=0)
    marks_buf[...] = marks
    copy = pltpu.make_async_copy(marks_buf, slots, sem)
    copy.start()
    fill = jnp.zeros((LANES - 2 * lines, LANES), jnp.int32)
    both = jnp.concatenate([marks] + power_rows + [fill], axis=0).astype(f32)
    columns = both.T
    mark_columns = columns.astype(jnp.int32)
    scale_columns = jnp.exp2(columns)
    mark_line = jnp.concatenate([marks[k : k + 1, :strip] for k in range(lines)], axis=1)
    power_line = jnp.concatenate([both[lines + k : lines + k + 1, :strip] for k in range(lines)], axis=1)
    scale_line = jnp.exp2(power_line)
    for s, ref in enumerate(got):
        code = ref[:room, :].astype(jnp.int32)
        upper = (code + 128) >> 8
        lower = code - upper * 256
        halves = jnp.concatenate([upper.astype(f32), lower.astype(f32)], axis=1)
        wide[s * room : (s + 1) * room, :] = halves.astype(bf16)
    return copy, lines, strip, mark_line, scale_line, mark_columns, scale_columns


def block_sums(block, strip, mark_line, scale_line, mark_columns, wide):
    same = [
        jnp.where(mark_columns[:strip, k : k + 1] == mark_line, scale_line, 0.0).astype(jnp.bfloat16) for k in block
    ]
    sums = jnp.dot(jnp.concatenate(same, axis=0), wide[...], preferred_element_type=jnp.float32)
    return sums[:, :LANES] * 256.0 + sums[:, LANES:]


def own_rows(k, strip, lines, scale_columns, wide):
    own = wide[k * strip : (k + 1) * strip, :].astype(jnp.float32)
    return (own[:, :LANES] * 256.0 + own[:, LANES:]) * scale_columns[:strip, lines + k : lines + k + 1]


def fold(product):
    return jnp.sum(product.reshape(product.shape[0] // 8, 8, LANES), axis=0)


def line_blocks(lines, strip):
    per_block = max(1, 256 // strip)
    return [range(k, min(k + per_block, lines)) for k in range(0, lines, per_block)]


def join_kernel(group, room, opens, ends, middle, *refs):
    got, refs = refs[:group], refs[group:]
    if not opens:
        (_, sum_ref), refs = refs[:2], refs[2:]
    if middle:
        state_hbm, grad_ref, part_ref, state_ref, *refs, state_sem = refs
        state_copy = pltpu.make_async_copy(state_hbm, state_ref, state_sem)
        state_copy.start()
    else:
        grad_ref, part_ref, *refs = refs
    wide, sums_buf, before_buf, marks_buf, slots, sem = refs
    if opens:
        grad_ref[...] = jnp.zeros_like(grad_ref)
    copy, lines, strip, mark_line, scale_line, mark_columns, scale_columns = open_blocks(
        got, room, marks_buf, slots, sem, wide
    )
    total = jnp.zeros((8, LANES), jnp.float32) if opens else sum_ref[...]
    if not opens:
        copy.wait()
        for k in range(lines):
            for r in range(strip):
                before_buf[k * strip + r : k * strip + r + 1, :] = grad_ref[pl.ds(slots[k, r], 1), :]
    for block in line_blocks(lines, strip):
        sums = block_sums(block, strip, mark_line, scale_line, mark_columns, wide)
        for n, k in enumerate(block):
            here = slice(k * strip, (k + 1) * strip)
            after = sums[n * strip : (n + 1) * strip]
            twice = after
            if not opens:
                before = before_buf[here, :]
                after = before + after
                twice = before + after
            sums_buf[here, :] = after
            total = total + fold(own_rows(k, strip, lines, scale_columns, wide) * twice)
        if opens and block[0] == 0:
            copy.wait()
        for k in block:
            for r in range(strip):
                grad_ref[pl.ds(slots[k, r], 1), :] = sums_buf[k * strip + r : k * strip + r + 1, :]
    if ends:
        total = jnp.sum(total, axis=0, keepdims=True)
        total = jnp.sum(total, axis=1, keepdims=True)
        part_ref[...] = jnp.broadcast_to(total[None], part_ref.shape)
    else:
        part_ref[...] = total
    if middle:
        state_copy.wait()


def update_kernel(limit, step, parts_ref, grad_ref, table_ref, first_ref, second_ref, table_out, first_out, second_out,
                  table_buf, first_buf, second_buf, sems):
    total = jnp.sum(parts_ref[...], axis=0)
    scale = limit / jnp.maximum(jnp.sqrt(total), limit)
    rows = table_ref.shape[0]
    copies = []
    for n in range(rows // step):
        part = pl.ds(n * step, step)
        clipped = scale * grad_ref[part, :]
        new_first = beta_first * first_ref[part, :] + (1.0 - beta_first) * clipped
        first_buf[part, :] = new_first
        new_second = beta_second * second_ref[part, :] + (1.0 - beta_second) * clipped * clipped
        second_buf[part, :] = new_second
        spread = new_second * (1.0 / second_fix)
        change = (new_first * (learn_rate / first_fix)) / (spread * lax.rsqrt(spread) + adam_eps)
        table_buf[part, :] = table_ref[part, :] * (1.0 - learn_rate * decay_rate) - change
        for k, (a, b) in enumerate(((first_buf, first_out), (second_buf, second_out), (table_buf, table_out))):
            copy = pltpu.make_async_copy(a.at[part], b.at[part], sems.at[k, n])
            copy.start()
            copies.append(copy)
    for copy in copies:
        copy.wait()


def body(table, first_moment, second_moment, grads, ids):
    peers = lax.axis_size("dp")
    everyone = peers * lax.axis_size("mp")
    rows_dev, width = table.shape
    tok_dev = grads.shape[0]
    room = tok_dev // peers
    strips = strip_rows(room)
    f32 = jnp.float32
    shape = jax.ShapeDtypeStruct
    vmem = pl.BlockSpec(memory_space=pltpu.VMEM)
    hbm = pl.BlockSpec(memory_space=pltpu.HBM)
    in_hbm = lambda x: pltpu.with_memory_space_constraint(x, pltpu.HBM)
    in_vmem = lambda x: pltpu.with_memory_space_constraint(x, pltpu.VMEM)
    kept = pltpu.VMEM((rows_dev, width), f32)
    dense = shape((rows_dev, width), f32)
    parcel = shape((room + META, width), jnp.int16)
    params = lambda mib: pltpu.CompilerParams(vmem_limit_bytes=mib * MIB)
    effort = lambda flops, moved: pl.CostEstimate(flops=flops, bytes_accessed=moved, transcendentals=0)
    near, far = peers // 2, peers - peers // 2
    line = pltpu.VMEM((1, tok_dev), jnp.int32)
    *packed_far, rel, rank, wide, table_kept = pl.pallas_call(
        functools.partial(pack_far_kernel, peers, rows_dev, room),
        out_shape=(parcel,) * far
        + (line, line, pltpu.VMEM((tok_dev, 2 * width), jnp.bfloat16), kept),
        in_specs=[hbm] * 3,
        out_specs=(vmem,) * (far + 4),
        scratch_shapes=[
            pltpu.VMEM((1, tok_dev), jnp.int32),
            pltpu.VMEM((tok_dev, width), jnp.bfloat16),
            pltpu.SemaphoreType.DMA((3,)),
        ],
        compiler_params=params(24),
        name="pack_far",
    )(*[in_hbm(x) for x in (ids.reshape(1, tok_dev), grads, table)])
    got = [None] * peers
    for hop in range(peers - 1, near - 1, -1):
        got[hop] = lax.ppermute(packed_far[hop - near], "dp", hop_pairs(hop, peers))
    *packed_near, second_kept = pl.pallas_call(
        functools.partial(pack_near_kernel, peers, rows_dev, room),
        out_shape=(parcel,) * near + (kept,),
        in_specs=[vmem, vmem, vmem, hbm],
        out_specs=(vmem,) * (near + 1),
        scratch_shapes=[pltpu.SemaphoreType.DMA],
        compiler_params=params(24),
        cost_estimate=effort(4 * tok_dev * near * room * width, 16 * rows_dev * width),
        name="pack_near",
    )(in_vmem(rel), in_vmem(rank), in_vmem(wide), in_hbm(second_moment))
    got[0] = packed_near[0]
    for hop in range(near - 1, 0, -1):
        got[hop] = lax.ppermute(packed_near[hop], "dp", hop_pairs(hop, peers))
    longer = pltpu.VMEM((rows_dev + 8, width), f32)

    lead, half, most = far // 4, far // 2, 3 * far // 4
    hops = [*range(near + far // 2, peers), *range(near + far // 2 - 1, 0, -1)]
    rounds = [[0, *hops[:lead]], [*hops[lead:most], *hops[far:]], hops[most:far]]
    grad_rows = part = None
    for n, members in enumerate(rounds):
        opens, ends = n == 0, n == len(rounds) - 1
        middle = n == 1
        group = len(members)
        operands = [got[hop] for hop in members]
        if not opens:
            operands += [in_vmem(grad_rows), part]
        if middle:
            operands.append(in_hbm(first_moment))
        grad_rows, part, *state = pl.pallas_call(
            functools.partial(join_kernel, group, room, opens, ends, middle),
            out_shape=(longer, shape((everyone, 1, width) if ends else (8, LANES), f32)) + (kept,) * middle,
            in_specs=[vmem] * (len(operands) - middle) + [hbm] * middle,
            out_specs=(vmem,) * (2 + middle),
            input_output_aliases={} if opens else {group: 0},
            scratch_shapes=[
                pltpu.VMEM((group * room, 2 * width), jnp.bfloat16),
                pltpu.VMEM((group * room, width), f32),
                pltpu.VMEM((group * room, width), f32),
                pltpu.VMEM((group * strips, LANES), jnp.int32),
                pltpu.SMEM((group * strips, LANES), jnp.int32),
                pltpu.SemaphoreType.DMA,
            ]
            + [pltpu.SemaphoreType.DMA] * middle,
            compiler_params=params(16),
            cost_estimate=effort(width, width),
            name="join_rows_%d" % n,
        )(*operands)
        if middle:
            (first_kept,) = state
    parts = lax.all_to_all(part, ("dp", "mp"), split_axis=0, concat_axis=0, tiled=True)
    limit = math.sqrt(tok_dev * everyone * width)
    step = math.gcd(1024, rows_dev)
    return pl.pallas_call(
        functools.partial(update_kernel, limit, step),
        out_shape=(dense,) * 3,
        in_specs=[vmem] * 5,
        out_specs=(hbm,) * 3,
        scratch_shapes=[pltpu.VMEM((rows_dev, width), f32)] * 3 + [pltpu.SemaphoreType.DMA((3, rows_dev // step))],
        compiler_params=params(20),
        name="update_rows",
    )(parts, *[in_vmem(x) for x in (grad_rows, table_kept, first_kept, second_kept)])


def solution(mesh):
    in_specs = (P("dp", "mp"), P("dp", "mp"), P("dp", "mp"), P("dp", "mp"), P("dp"))
    out_specs = (P("dp", "mp"), P("dp", "mp"), P("dp", "mp"))
    return jax.shard_map(body, mesh=mesh, in_specs=in_specs, out_specs=out_specs, check_vma=False)
```

```python
import functools
import math

import jax
import jax.numpy as jnp
from jax import lax
from jax.experimental import pallas as pl
from jax.experimental.pallas import tpu as pltpu
from jax.sharding import PartitionSpec as P

beta_first = 0.9
beta_second = 0.999
learn_rate = 0.01
decay_rate = 0.1
adam_eps = 1e-08
first_fix = 0.9999734386
second_fix = 0.0952078529

LANES = 128
META = 16
TOP = 32767.0
MIB = 2**20


def strip_rows(room):
    return -(-room // LANES)


def relative(me, owner, peers):
    return owner ^ me if peers & (peers - 1) == 0 else lax.rem(owner - me + peers, peers)


def hop_pairs(hop, peers):
    return [(i, i ^ hop if peers & (peers - 1) == 0 else (i + hop) % peers) for i in range(peers)]


def one_hot(keys, count):
    tall = 16 if count % 16 == 0 else count
    place = lax.broadcasted_iota(jnp.int32, (tall, keys.shape[1]), 0).astype(jnp.int16)
    keys = jnp.broadcast_to(keys, (tall, keys.shape[1])).astype(jnp.int16)
    one, zero = jnp.ones(keys.shape, jnp.bfloat16), jnp.zeros(keys.shape, jnp.bfloat16)
    return jnp.concatenate([jnp.where(place == keys - k, one, zero) for k in range(0, count, tall)], axis=0)


def rank_tables(group, per_owner):
    bf16 = jnp.bfloat16
    row = lax.broadcasted_iota(jnp.int32, (LANES, LANES), 0)
    column = lax.broadcasted_iota(jnp.int32, (LANES, LANES), 1)
    before = jnp.where(column < row, 1.0, 0.0).astype(bf16)
    ones = jnp.ones((LANES, LANES), bf16)
    source = lax.broadcasted_iota(jnp.int32, (per_owner, per_owner), 0)
    target = lax.broadcasted_iota(jnp.int32, (per_owner, per_owner), 1)
    ahead = jnp.where(source < target, 1.0, 0.0)
    blank = jnp.zeros((per_owner, per_owner), jnp.float32)
    rows = [jnp.concatenate([ahead if k == o else blank for k in range(group)], axis=1) for o in range(group)]
    return before, ones, jnp.concatenate(rows, axis=0).astype(bf16)


def slot_ranks(rel, tables):
    f32, bf16 = jnp.float32, jnp.bfloat16
    before, ones, ahead = tables
    high_hot = one_hot(rel >> 7, ahead.shape[0])
    low_hot = one_hot(rel & (LANES - 1), LANES)
    counts = lax.dot_general(low_hot, high_hot, (((1,), (1,)), ((), ())), preferred_element_type=f32)
    present = jnp.where(counts > 0.0, 1.0, 0.0).astype(bf16)
    within = jnp.dot(before, present, preferred_element_type=f32)
    totals = jnp.dot(ones, present, preferred_element_type=f32).astype(bf16)
    ranks = within + jnp.dot(totals, ahead, preferred_element_type=f32)
    by_low = jnp.dot(ranks.astype(bf16), high_hot, preferred_element_type=f32)
    return jnp.sum(by_low * low_hot.astype(f32), axis=0, keepdims=True).astype(jnp.int32)


def pack_group(rel, rank, wide, first, outs, rows_dev, room):
    f32 = jnp.float32
    group = len(outs)
    strips = strip_rows(room)
    lane = lax.broadcasted_iota(jnp.int32, (room, LANES), 1)
    meta = jnp.zeros((room, LANES), f32)
    for o in range(group):
        inside = jnp.logical_and(rel >= (first + o) * rows_dev, rel < (first + o + 1) * rows_dev)
        match = one_hot(jnp.where(inside, rank, -1), room)
        summed = jnp.dot(match, wide, preferred_element_type=f32)
        sums = summed[:, :LANES]
        digit_high = summed[:, LANES : LANES + 1]
        digit_low = summed[:, LANES + 1 : LANES + 2]
        number = summed[:, LANES + 2 : LANES + 3]
        mark = jnp.where(
            number > 0.0,
            jnp.floor((digit_high * LANES + digit_low) / jnp.maximum(number, 1.0) + 0.5),
            float(rows_dev),
        )
        largest = jnp.max(jnp.abs(sums), axis=1, keepdims=True)
        power = jnp.ceil(jnp.log2(jnp.maximum(largest, 1e-30) * (1.0 / TOP)))
        code = jnp.clip(jnp.round(sums * jnp.exp2(-power)), -TOP, TOP)
        outs[o][:room, :] = code.astype(jnp.int32).astype(jnp.int16)
        meta = jnp.where(lane == 2 * o, mark, jnp.where(lane == 2 * o + 1, power, meta))
    flat = meta.T.astype(jnp.int32)
    for o in range(group):
        rows = []
        for k in range(2):
            for c in range(strips):
                piece = flat[2 * o + k : 2 * o + k + 1, c * LANES : min((c + 1) * LANES, room)]
                if piece.shape[1] < LANES:
                    piece = jnp.concatenate([piece, jnp.zeros((1, LANES - piece.shape[1]), jnp.int32)], axis=1)
                rows.append(piece)
        rows.append(jnp.zeros((META - len(rows), LANES), jnp.int32))
        outs[o][room:, :] = jnp.concatenate(rows, axis=0).astype(jnp.int16)


def low_part(ids, size):
    return ids & (size - 1) if size & (size - 1) == 0 else lax.rem(ids, size)


def relative_rows(ids, peers, rows_dev):
    me = lax.axis_index("dp")
    if rows_dev & (rows_dev - 1) == 0 and peers & (peers - 1) == 0:
        return ids ^ (me * rows_dev)
    owner = ids // rows_dev
    return relative(me, owner, peers) * rows_dev + (ids - owner * rows_dev)


def pack_far_kernel(peers, rows_dev, room, ids_hbm, grads_hbm, table_hbm, *refs):
    far = peers - peers // 2
    outs, refs = refs[:far], refs[far:]
    rel_ref, rank_ref, wide_ref, table_ref, ids_ref, grads_ref, sems = refs
    pairs = ((ids_hbm, ids_ref), (grads_hbm, grads_ref), (table_hbm, table_ref))
    copies = [pltpu.make_async_copy(a, b, sems.at[n]) for n, (a, b) in enumerate(pairs)]
    copies[0].start()
    copies[1].start()
    tables = rank_tables(peers, rows_dev // LANES)
    copies[0].wait()
    for copy in copies[2:]:
        copy.start()
    rel = relative_rows(ids_ref[...], peers, rows_dev)
    tok = rel.shape[1]
    rank = slot_ranks(rel, tables)
    rel_ref[...] = rel
    rank_ref[...] = rank
    sub = lax.broadcasted_iota(jnp.int32, (8, tok), 0)
    high = low_part(rel, rows_dev) >> 7
    low = rel & (LANES - 1)
    digits = jnp.where(sub == 0, high, jnp.where(sub == 1, low, jnp.where(sub == 2, 1, 0))).astype(jnp.float32)
    aux = []
    for c in range(tok // LANES):
        tile = digits[:, c * LANES : (c + 1) * LANES]
        tile = jnp.concatenate([tile, jnp.zeros((LANES - 8, LANES), jnp.float32)], axis=0)
        aux.append(tile.T)
    copies[1].wait()
    wide = jnp.concatenate([grads_ref[...], jnp.concatenate(aux, axis=0).astype(jnp.bfloat16)], axis=1)
    wide_ref[...] = wide
    pack_group(rel, rank, wide, peers // 2, outs, rows_dev, room)
    for copy in copies[2:]:
        copy.wait()


def pack_near_kernel(peers, rows_dev, room, rel_ref, rank_ref, wide_ref, second_hbm, *refs):
    outs, (second_ref, sem) = refs[: peers // 2], refs[peers // 2 :]
    copy = pltpu.make_async_copy(second_hbm, second_ref, sem)
    copy.start()
    pack_group(rel_ref[...], rank_ref[...], wide_ref[...], 0, outs, rows_dev, room)
    copy.wait()


def open_blocks(got, room, marks_buf, slots, sem, wide):
    strips = strip_rows(room)
    f32, bf16 = jnp.float32, jnp.bfloat16
    lines = len(got) * strips
    strip = min(room, LANES)
    mark_rows, power_rows = [], []
    for ref in got:
        meta = ref[room:, :].astype(jnp.int32)
        mark_rows.append(meta[0:strips])
        power_rows.append(meta[strips : 2 * strips])
    marks = jnp.concatenate(mark_rows, axis=0)
    marks_buf[...] = marks
    copy = pltpu.make_async_copy(marks_buf, slots, sem)
    copy.start()
    fill = jnp.zeros((LANES - 2 * lines, LANES), jnp.int32)
    both = jnp.concatenate([marks] + power_rows + [fill], axis=0).astype(f32)
    columns = both.T
    mark_columns = columns.astype(jnp.int32)
    scale_columns = jnp.exp2(columns)
    mark_line = jnp.concatenate([marks[k : k + 1, :strip] for k in range(lines)], axis=1)
    power_line = jnp.concatenate([both[lines + k : lines + k + 1, :strip] for k in range(lines)], axis=1)
    scale_line = jnp.exp2(power_line)
    for s, ref in enumerate(got):
        code = ref[:room, :].astype(jnp.int32)
        upper = (code + 128) >> 8
        lower = code - upper * 256
        halves = jnp.concatenate([upper.astype(f32), lower.astype(f32)], axis=1)
        wide[s * room : (s + 1) * room, :] = halves.astype(bf16)
    return copy, lines, strip, mark_line, scale_line, mark_columns, scale_columns


def block_sums(block, strip, mark_line, scale_line, mark_columns, wide):
    same = [
        jnp.where(mark_columns[:strip, k : k + 1] == mark_line, scale_line, 0.0).astype(jnp.bfloat16) for k in block
    ]
    sums = jnp.dot(jnp.concatenate(same, axis=0), wide[...], preferred_element_type=jnp.float32)
    return sums[:, :LANES] * 256.0 + sums[:, LANES:]


def own_rows(k, strip, lines, scale_columns, wide):
    own = wide[k * strip : (k + 1) * strip, :].astype(jnp.float32)
    return (own[:, :LANES] * 256.0 + own[:, LANES:]) * scale_columns[:strip, lines + k : lines + k + 1]


def fold(product):
    return jnp.sum(product.reshape(product.shape[0] // 8, 8, LANES), axis=0)


def line_blocks(lines, strip):
    per_block = max(1, 256 // strip)
    return [range(k, min(k + per_block, lines)) for k in range(0, lines, per_block)]


def join_kernel(group, room, opens, ends, middle, *refs):
    got, refs = refs[:group], refs[group:]
    if not opens:
        (_, sum_ref), refs = refs[:2], refs[2:]
    if middle:
        state_hbm, grad_ref, part_ref, state_ref, *refs, state_sem = refs
        state_copy = pltpu.make_async_copy(state_hbm, state_ref, state_sem)
        state_copy.start()
    else:
        grad_ref, part_ref, *refs = refs
    wide, sums_buf, before_buf, marks_buf, slots, sem = refs
    if opens:
        grad_ref[...] = jnp.zeros_like(grad_ref)
    copy, lines, strip, mark_line, scale_line, mark_columns, scale_columns = open_blocks(
        got, room, marks_buf, slots, sem, wide
    )
    total = jnp.zeros((8, LANES), jnp.float32) if opens else sum_ref[...]
    if not opens:
        copy.wait()
        for k in range(lines):
            for r in range(strip):
                before_buf[k * strip + r : k * strip + r + 1, :] = grad_ref[pl.ds(slots[k, r], 1), :]
    for block in line_blocks(lines, strip):
        sums = block_sums(block, strip, mark_line, scale_line, mark_columns, wide)
        for n, k in enumerate(block):
            here = slice(k * strip, (k + 1) * strip)
            after = sums[n * strip : (n + 1) * strip]
            twice = after
            if not opens:
                before = before_buf[here, :]
                after = before + after
                twice = before + after
            sums_buf[here, :] = after
            total = total + fold(own_rows(k, strip, lines, scale_columns, wide) * twice)
        if opens and block[0] == 0:
            copy.wait()
        for k in block:
            for r in range(strip):
                grad_ref[pl.ds(slots[k, r], 1), :] = sums_buf[k * strip + r : k * strip + r + 1, :]
    if ends:
        total = jnp.sum(total, axis=0, keepdims=True)
        total = jnp.sum(total, axis=1, keepdims=True)
        part_ref[...] = jnp.broadcast_to(total[None], part_ref.shape)
    else:
        part_ref[...] = total
    if middle:
        state_copy.wait()


def update_kernel(limit, step, parts_ref, grad_ref, table_ref, first_ref, second_ref, table_out, first_out, second_out,
                  table_buf, first_buf, second_buf, sems):
    total = jnp.sum(parts_ref[...], axis=0)
    scale = limit / jnp.maximum(jnp.sqrt(total), limit)
    rows = table_ref.shape[0]
    copies = []
    cuts = [0, step // 4, *range(step, rows + 1, step)]
    for n, (low, high) in enumerate(zip(cuts, cuts[1:])):
        part = pl.ds(low, high - low)
        clipped = scale * grad_ref[part, :]
        new_first = beta_first * first_ref[part, :] + (1.0 - beta_first) * clipped
        first_buf[part, :] = new_first
        new_second = beta_second * second_ref[part, :] + (1.0 - beta_second) * clipped * clipped
        second_buf[part, :] = new_second
        spread = new_second * (1.0 / second_fix)
        change = (new_first * (learn_rate / first_fix)) / (spread * lax.rsqrt(spread) + adam_eps)
        table_buf[part, :] = table_ref[part, :] * (1.0 - learn_rate * decay_rate) - change
        for k, (a, b) in enumerate(((first_buf, first_out), (second_buf, second_out), (table_buf, table_out))):
            copy = pltpu.make_async_copy(a.at[part], b.at[part], sems.at[k, n])
            copy.start()
            copies.append(copy)
    for copy in copies:
        copy.wait()


def body(table, first_moment, second_moment, grads, ids):
    peers = lax.axis_size("dp")
    everyone = peers * lax.axis_size("mp")
    rows_dev, width = table.shape
    tok_dev = grads.shape[0]
    room = tok_dev // peers
    strips = strip_rows(room)
    f32 = jnp.float32
    shape = jax.ShapeDtypeStruct
    vmem = pl.BlockSpec(memory_space=pltpu.VMEM)
    hbm = pl.BlockSpec(memory_space=pltpu.HBM)
    in_hbm = lambda x: pltpu.with_memory_space_constraint(x, pltpu.HBM)
    in_vmem = lambda x: pltpu.with_memory_space_constraint(x, pltpu.VMEM)
    kept = pltpu.VMEM((rows_dev, width), f32)
    dense = shape((rows_dev, width), f32)
    parcel = shape((room + META, width), jnp.int16)
    params = lambda mib: pltpu.CompilerParams(vmem_limit_bytes=mib * MIB)
    effort = lambda flops, moved: pl.CostEstimate(flops=flops, bytes_accessed=moved, transcendentals=0)
    near, far = peers // 2, peers - peers // 2
    line = pltpu.VMEM((1, tok_dev), jnp.int32)
    *packed_far, rel, rank, wide, table_kept = pl.pallas_call(
        functools.partial(pack_far_kernel, peers, rows_dev, room),
        out_shape=(parcel,) * far
        + (line, line, pltpu.VMEM((tok_dev, 2 * width), jnp.bfloat16), kept),
        in_specs=[hbm] * 3,
        out_specs=(vmem,) * (far + 4),
        scratch_shapes=[
            pltpu.VMEM((1, tok_dev), jnp.int32),
            pltpu.VMEM((tok_dev, width), jnp.bfloat16),
            pltpu.SemaphoreType.DMA((3,)),
        ],
        compiler_params=params(24),
        name="pack_far",
    )(*[in_hbm(x) for x in (ids.reshape(1, tok_dev), grads, table)])
    got = [None] * peers
    for hop in range(peers - 1, near - 1, -1):
        got[hop] = lax.ppermute(packed_far[hop - near], "dp", hop_pairs(hop, peers))
    *packed_near, second_kept = pl.pallas_call(
        functools.partial(pack_near_kernel, peers, rows_dev, room),
        out_shape=(parcel,) * near + (kept,),
        in_specs=[vmem, vmem, vmem, hbm],
        out_specs=(vmem,) * (near + 1),
        scratch_shapes=[pltpu.SemaphoreType.DMA],
        compiler_params=params(24),
        cost_estimate=effort(4 * tok_dev * near * room * width, 16 * rows_dev * width),
        name="pack_near",
    )(in_vmem(rel), in_vmem(rank), in_vmem(wide), in_hbm(second_moment))
    got[0] = packed_near[0]
    for hop in range(near - 1, 0, -1):
        got[hop] = lax.ppermute(packed_near[hop], "dp", hop_pairs(hop, peers))
    longer = pltpu.VMEM((rows_dev + 8, width), f32)

    lead, half, most = far // 4, far // 2, 3 * far // 4
    hops = [*range(near + far // 2, peers), *range(near + far // 2 - 1, 0, -1)]
    rounds = [[0, *hops[:lead]], [*hops[lead:most], *hops[far:]], hops[most:far]]
    grad_rows = part = None
    for n, members in enumerate(rounds):
        opens, ends = n == 0, n == len(rounds) - 1
        middle = n == 1
        group = len(members)
        operands = [got[hop] for hop in members]
        if not opens:
            operands += [in_vmem(grad_rows), part]
        if middle:
            operands.append(in_hbm(first_moment))
        grad_rows, part, *state = pl.pallas_call(
            functools.partial(join_kernel, group, room, opens, ends, middle),
            out_shape=(longer, shape((everyone, 1, width) if ends else (8, LANES), f32)) + (kept,) * middle,
            in_specs=[vmem] * (len(operands) - middle) + [hbm] * middle,
            out_specs=(vmem,) * (2 + middle),
            input_output_aliases={} if opens else {group: 0},
            scratch_shapes=[
                pltpu.VMEM((group * room, 2 * width), jnp.bfloat16),
                pltpu.VMEM((group * room, width), f32),
                pltpu.VMEM((group * room, width), f32),
                pltpu.VMEM((group * strips, LANES), jnp.int32),
                pltpu.SMEM((group * strips, LANES), jnp.int32),
                pltpu.SemaphoreType.DMA,
            ]
            + [pltpu.SemaphoreType.DMA] * middle,
            compiler_params=params(16),
            cost_estimate=effort(width, width),
            name="join_rows_%d" % n,
        )(*operands)
        if middle:
            (first_kept,) = state
    parts = lax.all_to_all(part, ("dp", "mp"), split_axis=0, concat_axis=0, tiled=True)
    limit = math.sqrt(tok_dev * everyone * width)
    step = math.gcd(1024, rows_dev)
    return pl.pallas_call(
        functools.partial(update_kernel, limit, step),
        out_shape=(dense,) * 3,
        in_specs=[vmem] * 5,
        out_specs=(hbm,) * 3,
        scratch_shapes=[pltpu.VMEM((rows_dev, width), f32)] * 3 + [pltpu.SemaphoreType.DMA((3, rows_dev // step + 1))],
        compiler_params=params(20),
        name="update_rows",
    )(parts, *[in_vmem(x) for x in (grad_rows, table_kept, first_kept, second_kept)])


def solution(mesh):
    in_specs = (P("dp", "mp"), P("dp", "mp"), P("dp", "mp"), P("dp", "mp"), P("dp"))
    out_specs = (P("dp", "mp"), P("dp", "mp"), P("dp", "mp"))
    return jax.shard_map(body, mesh=mesh, in_specs=in_specs, out_specs=out_specs, check_vma=False)
```
